32 devices in a mesh: filt: 16 (over z, y, core), space: 2 (over x).
Axes of the slice: x: 2, y: 2, z: 4, core: 2. Of those that a mesh axis runs over, the one named last changes fastest.
Arguments:
- volume: bfloat16 [256, 8, 4, 128], P('filt', 'space'), may hold values from -6 to 6
- kernel: bfloat16 [512, 3, 3, 3, 256], P('filt'), may hold values from -0.078125 to 0.078125
- filter_bias: bfloat16 [512], P('filt'), may hold values from -3 to 3
Outputs:
- pooled: bfloat16 [512, 4, 2, 64], P('filt', 'space')
The draws below stay inside these ranges and needn't reach their ends.
All inputs are finite; a program needn't handle non-finite values.
Results may differ from the reference program's by a relative error of at most 0.001.
Values may be sent and summed in bfloat16 or wider, within the bound.
No kernel may reach another device: no remote copies, remote signals or barrier semaphores. Data moves between devices by JAX's collectives and lax.ppermute only.
A program may use at most 64 MiB of HBM per device.

```python
import jax
import jax.numpy as jnp
from jax import lax

CIN = 256
COUT = 512
NY = 4
NX = 128
NZ = 8


def block_scale(rng, extent, pieces, least, largest):
    gain = 1.0
    for dim, blocks in pieces:
        draws = jax.random.uniform(jax.random.fold_in(jax.random.fold_in(rng, 6), dim), (blocks,), jnp.float32, least / len(pieces), largest / len(pieces))
        gain = gain * jnp.repeat(jnp.exp(draws), extent[dim] // blocks).reshape((-1,) + (1,) * (len(extent) - 1 - dim))
    return gain


def bell_draw(own_key, dims, deviation, reach, split=(), held_as=jnp.bfloat16):
    level = block_scale(own_key, dims, split, -0.22, 0.18) if split else 1.0
    result = jax.random.normal(own_key, dims, jnp.float32) * deviation * level
    return jnp.minimum(jnp.maximum(result, -reach), reach).astype(held_as)


def setup_inputs(seed: int = 0) -> dict:
    splits = jax.random.split(jax.random.key(seed), 4)
    return {
        "volume": bell_draw(splits[0], (CIN, NZ, NY, NX), 1.0, 6.0, ((0, 16), (1, 2))),
        "kernel": bell_draw(splits[1], (COUT, 3, 3, 3, CIN), (27 * CIN) ** -0.5, 0.078125, ((0, 16),)),
        "filter_bias": bell_draw(splits[2], (COUT,), 0.5, 3.0, ((0, 16),)),
    }


slope = 0.3


def reference(volume, kernel, filter_bias):
    inputs = volume.astype(jnp.float32)[None]
    weights = kernel.astype(jnp.float32)
    summed = lax.conv_general_dilated(inputs, weights, (1, 1, 1), ((1, 1), (1, 1), (1, 1)), dimension_numbers=("NCDHW", "ODHWI", "NCDHW"), precision=lax.Precision.HIGHEST)[0]
    activated = summed + filter_bias.astype(jnp.float32)[:, None, None, None]
    activated = jnp.where(activated > 0, activated, slope * activated)
    filters, depth, height, across = activated.shape
    blocked = activated.reshape(filters, depth // 2, 2, height // 2, 2, across // 2, 2)
    return jnp.max(blocked, axis=(2, 4, 6)).astype(jnp.bfloat16)
```

```python
import jax
import jax.numpy as jnp
from jax import lax
from jax.experimental import pallas as pl
from jax.experimental.pallas import tpu as pltpu
from jax.sharding import PartitionSpec as P

slope = 0.3
f32, bf16 = jnp.float32, jnp.bfloat16


def boundary_planes(volume):
    count = lax.axis_size("space")
    depth = volume.shape[1]
    first = lax.slice_in_dim(volume, 0, 1, axis=1)
    last = lax.slice_in_dim(volume, depth - 1, depth, axis=1)
    if count == 2:
        here = lax.axis_index("space")
        got = lax.ppermute(jnp.where(here == 0, last, first), "space", [(0, 1), (1, 0)])
        return [got]
    forward = [(i, i + 1) for i in range(count - 1)]
    low = lax.ppermute(last, "space", forward)
    high = lax.ppermute(first, "space", [(t, s) for s, t in forward])
    return [low, high]


def rows_of(ref, row):
    return jnp.concatenate([ref[k, row] for k in range(ref.shape[0])], axis=0)


def make_padded(vol_ref, pad_ref, flags_ref, depth, height):
    across = vol_ref.shape[-1]
    channels = pad_ref.shape[1]
    extra = vol_ref.shape[1] // height - depth
    zero = jnp.zeros((channels, across), bf16)
    for plane in range(depth + 2):
        pad_ref[plane, :, 0:across] = zero
        pad_ref[plane, :, (height + 1) * across :] = zero
        for y in range(height):
            if 1 <= plane <= depth:
                rows = rows_of(vol_ref, (plane - 1) * height + y)
            else:
                which = 0 if plane == 0 or extra == 1 else 1
                rows = rows_of(vol_ref, (depth + which) * height + y)
                keep = flags_ref[1 if plane == 0 else 2]
                rows = jnp.where(keep > 0, rows, zero)
            pad_ref[plane, :, (y + 1) * across : (y + 2) * across] = rows


def taps_product(weights, pad_ref, z, y, across):
    left = jnp.concatenate([weights[a][b] for a in range(3) for b in range(3)], axis=1)
    right = jnp.concatenate(
        [
            pad_ref[z + a, :, (y + b) * across : (y + b + 2) * across]
            for a in range(3)
            for b in range(3)
        ],
        axis=0,
    )
    return jnp.dot(left, right, preferred_element_type=f32)


def own_half(flags_ref, w_ref, vol_ref, sum_ref, w_out_ref, pad_ref, *, depth, height, block):
    across = vol_ref.shape[-1]
    cin = w_ref.shape[1]
    half = cin // 2
    core = flags_ref[0]
    source = lax.broadcasted_iota(jnp.int32, (cin, cin), 0)
    target = lax.broadcasted_iota(jnp.int32, (cin, cin), 1)
    place = target & (half - 1)
    part = jnp.where(target < half, core, 1 - core)
    wanted = ((place & ~(block - 1)) << 1) + part * block + (place & (block - 1))
    shuffle = jnp.where(source == wanted, 1.0, 0.0).astype(bf16)
    ordered = jnp.dot(w_ref[...], shuffle, preferred_element_type=f32).astype(bf16)
    w_out_ref[...] = ordered[:, half:]
    rows = w_ref.shape[0] // 9
    weights = [
        [ordered[(a * 3 + b) * rows : (a * 3 + b + 1) * rows, :half] for b in range(3)]
        for a in range(3)
    ]
    make_padded(vol_ref, pad_ref, flags_ref, depth, height)
    for z in range(depth):
        for y in range(0, height, 2):
            sum_ref[z * (height // 2) + y // 2] = taps_product(weights, pad_ref, z, y, across)


def other_half(flags_ref, w_ref, vol_ref, sum_ref, bias_ref, out_ref, pad_ref, *, depth, height):
    across = vol_ref.shape[-1]
    rows = w_ref.shape[0] // 9
    filters = rows // 3
    weights = [
        [w_ref[(a * 3 + b) * rows : (a * 3 + b + 1) * rows] for b in range(3)] for a in range(3)
    ]
    make_padded(vol_ref, pad_ref, flags_ref, depth, height)
    lane = lax.broadcasted_iota(jnp.int32, (filters, across), 1)
    bias = bias_ref[...]
    pooled = {}
    for z in range(depth):
        for y in range(0, height, 2):
            total = taps_product(weights, pad_ref, z, y, across)
            total += sum_ref[z * (height // 2) + y // 2]
            for k in range(2):
                part = total[:, k * across : (k + 1) * across]
                left = pltpu.roll(part[:filters], 1, 1)
                right = pltpu.roll(part[2 * filters :], across - 1, 1)
                v = part[filters : 2 * filters] + bias
                v += jnp.where(lane > 0, left, 0.0)
                v += jnp.where(lane < across - 1, right, 0.0)
                v = jnp.where(v > 0, v, slope * v)
                key = (z // 2, y // 2)
                pooled[key] = v if key not in pooled else jnp.maximum(pooled[key], v)
    stacked = jnp.concatenate(
        [pooled[z, y] for z in range(depth // 2) for y in range(height // 2)], axis=0
    )
    stacked = jnp.maximum(stacked, pltpu.roll(stacked, across - 1, 1)).astype(bf16)
    cells = (depth // 2) * (height // 2)
    count = cells * filters
    target = lax.broadcasted_iota(jnp.int32, (count, count), 0)
    source = lax.broadcasted_iota(jnp.int32, (count, count), 1)
    wanted = (target & (cells - 1)) * filters + target // cells
    rows_pick = jnp.where(source == wanted, 1.0, 0.0).astype(bf16)
    lane_from = lax.broadcasted_iota(jnp.int32, (across, across // 2), 0)
    lane_to = lax.broadcasted_iota(jnp.int32, (across, across // 2), 1)
    lanes_pick = jnp.where(lane_from == 2 * lane_to, 1.0, 0.0).astype(bf16)
    picked = jnp.dot(stacked, lanes_pick, preferred_element_type=f32).astype(bf16)
    out_ref[...] = jnp.dot(rows_pick, picked, preferred_element_type=f32).astype(bf16)


def on_device(volume, kernel, filter_bias):
    block, depth, height, across = volume.shape
    filters, cin = kernel.shape[0], kernel.shape[-1]
    count = lax.axis_size("filt")
    spaces = lax.axis_size("space")
    here = lax.axis_index("space")
    core = lax.axis_index("filt") % 2
    flags = jnp.stack([core, here, spaces - 1 - here]).astype(jnp.int32)

    planes = jnp.concatenate([volume] + boundary_planes(volume), axis=1)
    planes = planes.transpose(1, 2, 0, 3).reshape(-1, block, across)
    same_core = [[2 * i + c for i in range(count // 2)] for c in range(2)]
    copies = jnp.broadcast_to(planes[None], (count // 2,) + planes.shape)
    mine = lax.all_to_all(copies, "filt", 0, 0, axis_index_groups=same_core)
    theirs = lax.ppermute(mine, "filt", [(i, i ^ 1) for i in range(count)])

    bias = jnp.broadcast_to(filter_bias.astype(f32)[:, None], (filters, across))
    weights = kernel.transpose(1, 2, 3, 0, 4).reshape(27 * filters, cin)
    vmem = pl.BlockSpec(memory_space=pltpu.VMEM)
    smem = pl.BlockSpec(memory_space=pltpu.SMEM)
    padded = pltpu.VMEM((depth + 2, cin // 2, (height + 2) * across), bf16)
    sums = (depth * height // 2, 3 * filters, 2 * across)
    params = pltpu.CompilerParams(vmem_limit_bytes=24 << 20)
    flops = 27 * filters * cin * depth * height * across

    def own(flags_ref, w_ref, vol_ref, sum_ref, w_out_ref, pad_ref):
        own_half(
            flags_ref, w_ref, vol_ref, sum_ref, w_out_ref, pad_ref,
            depth=depth, height=height, block=block,
        )

    def other(flags_ref, w_ref, vol_ref, sum_ref, bias_ref, out_ref, pad_ref):
        other_half(
            flags_ref, w_ref, vol_ref, sum_ref, bias_ref, out_ref, pad_ref,
            depth=depth, height=height,
        )

    partial, w_other = pl.pallas_call(
        own,
        out_shape=(
            jax.ShapeDtypeStruct(sums, f32),
            jax.ShapeDtypeStruct((27 * filters, cin // 2), bf16),
        ),
        in_specs=[smem, vmem, vmem],
        out_specs=(vmem, vmem),
        scratch_shapes=[padded],
        compiler_params=params,
        cost_estimate=pl.CostEstimate(flops=flops, bytes_accessed=2 << 20, transcendentals=0),
    )(flags, weights, mine)
    pooled = pl.pallas_call(
        other,
        out_shape=jax.ShapeDtypeStruct((filters * depth * height // 4, across // 2), bf16),
        in_specs=[smem, vmem, vmem, vmem, vmem],
        out_specs=vmem,
        scratch_shapes=[padded],
        compiler_params=params,
        cost_estimate=pl.CostEstimate(flops=flops, bytes_accessed=2 << 20, transcendentals=0),
    )(flags, w_other, theirs, partial, bias)
    return pooled.reshape(filters, depth // 2, height // 2, across // 2)


def solution(mesh):
    in_specs = (P("filt", "space", None, None), P("filt", None, None, None, None), P("filt"))
    out_specs = P("filt", "space", None, None)
    return jax.shard_map(
        on_device, mesh=mesh, in_specs=in_specs, out_specs=out_specs, check_vma=False
    )
```

```python
import functools

import jax
import jax.numpy as jnp
from jax import lax
from jax.experimental import pallas as pl
from jax.experimental.pallas import tpu as pltpu
from jax.sharding import PartitionSpec as P

slope = 0.3
f32, bf16 = jnp.float32, jnp.bfloat16


def prepare(flags_ref, kernel_ref, bias_ref, w_mine_ref, w_theirs_ref, bias_out_ref, *, block):
    cin = kernel_ref.shape[-1]
    half = cin // 2
    core, group = flags_ref[0], flags_ref[1]
    source = lax.broadcasted_iota(jnp.int32, (cin, cin), 0)
    target = lax.broadcasted_iota(jnp.int32, (cin, cin), 1)
    place = target & (half - 1)
    part = jnp.where(target < half, core, 1 - core)
    wanted = (((place // block) ^ group) * 2 + part) * block + (place & (block - 1))
    shuffle = jnp.where(source == wanted, 1.0, 0.0).astype(bf16)
    ordered = jnp.dot(kernel_ref[...], shuffle, preferred_element_type=f32).astype(bf16)
    w_mine_ref[...] = ordered[:, :half].reshape(w_mine_ref.shape)
    w_theirs_ref[...] = ordered[:, half:].reshape(w_theirs_ref.shape)
    filters = bias_ref.shape[1]
    row = lax.broadcasted_iota(jnp.int32, (filters, filters), 0)
    column = lax.broadcasted_iota(jnp.int32, (filters, filters), 1)
    spread = jnp.where(row == column, bias_ref[...].astype(f32), 0.0)
    bias_out_ref[...] = jnp.broadcast_to(
        jnp.sum(spread, axis=1, keepdims=True), bias_out_ref.shape
    )


def rows_of(ref, row):
    return jnp.concatenate([ref[k, row] for k in range(ref.shape[0])], axis=0)


def pad_rows(rows):
    zero = jnp.zeros_like(rows[0])
    return jnp.concatenate([zero] + rows + [zero], axis=1)


def interior(w_ref, vol_ref, pad_ref, z, y, depth, height):
    across = vol_ref.shape[-1]
    taps = [(a, b) for a in range(3) for b in range(3) if 0 <= z + a - 1 < depth]
    left = jnp.concatenate([w_ref[a * 3 + b] for a, b in taps], axis=1)
    right = jnp.concatenate(
        [pad_ref[z + a - 1, :, (y + b) * across : (y + b + 2) * across] for a, b in taps], axis=0
    )
    return jnp.dot(left, right, preferred_element_type=f32)


def fill_pad(vol_ref, pad_ref, depth, height):
    for z in range(depth):
        pad_ref[z] = pad_rows([rows_of(vol_ref, z * height + y) for y in range(height)])


def boundary(w_ref, vol_ref, plane, tap, y, height):
    across = vol_ref.shape[-1]
    rows = [rows_of(vol_ref, plane * height + k) for k in range(height)]
    padded = pad_rows(rows)
    left = jnp.concatenate([w_ref[tap * 3 + b] for b in range(3)], axis=1)
    right = jnp.concatenate(
        [padded[:, (y + b) * across : (y + b + 2) * across] for b in range(3)], axis=0
    )
    return jnp.dot(left, right, preferred_element_type=f32)


def combine(total, k, filters, across):
    part = total[:, k * across : (k + 1) * across]
    lane = lax.broadcasted_iota(jnp.int32, (filters, across), 1)
    left = pltpu.roll(part[:filters], 1, 1)
    right = pltpu.roll(part[2 * filters :], across - 1, 1)
    v = part[filters : 2 * filters]
    v += jnp.where(lane > 0, left, 0.0)
    return v + jnp.where(lane < across - 1, right, 0.0)


def edges_of(flags_ref, count, depth):
    if count == 2:
        up = flags_ref[2] == 0
        return [(jnp.where(up, depth - 1, 0), jnp.where(up, 0, 2))]
    return [(depth - 1, 0), (0, 2)]


def first_half(
    flags_ref, w_ref, vol_ref, sum_ref, edge_ref, pad_ref, *, depth, height, count
):
    fill_pad(vol_ref, pad_ref, depth, height)
    pairs = height // 2
    for k, (plane, tap) in enumerate(edges_of(flags_ref, count, depth)):
        for y in range(pairs):
            edge_ref[k * pairs + y] = boundary(w_ref, vol_ref, plane, tap, 2 * y, height)
    for z in range(depth):
        for y in range(pairs):
            sum_ref[z * pairs + y] = interior(w_ref, vol_ref, pad_ref, z, 2 * y, depth, height)


def send_edges(flags_ref, w_ref, vol_ref, edge_ref, out_ref, *, depth, height, count):
    across = vol_ref.shape[-1]
    filters = out_ref.shape[2]
    pairs = height // 2
    for k, (plane, tap) in enumerate(edges_of(flags_ref, count, depth)):
        for y in range(pairs):
            total = boundary(w_ref, vol_ref, plane, tap, 2 * y, height)
            total += edge_ref[k * pairs + y]
            for j in range(2):
                out_ref[k, 2 * y + j] = combine(total, j, filters, across)


def second_half(w_ref, vol_ref, sum_ref, bias_ref, out_ref, pad_ref, *, depth, height):
    across = vol_ref.shape[-1]
    filters = bias_ref.shape[0]
    pairs = height // 2
    fill_pad(vol_ref, pad_ref, depth, height)
    for z in range(depth):
        for y in range(pairs):
            total = interior(w_ref, vol_ref, pad_ref, z, 2 * y, depth, height)
            total += sum_ref[z * pairs + y]
            for j in range(2):
                v = combine(total, j, filters, across) + bias_ref[...]
                out_ref[z * height + 2 * y + j] = v


def finish(flags_ref, v_ref, *refs, depth, height, count):
    got_refs, out_ref = refs[:-1], refs[-1]
    filters, across = v_ref.shape[1:]
    pooled = {}
    for z in range(depth):
        for y in range(height):
            v = v_ref[z * height + y]
            if z == 0:
                beside = got_refs[0][0, y]
                v += jnp.where(flags_ref[2] > 0, beside, 0.0)
            if z == depth - 1:
                beside = got_refs[-1][0, y]
                v += jnp.where(flags_ref[3] > 0, beside, 0.0)
            v = jnp.where(v > 0, v, slope * v)
            key = (z // 2, y // 2)
            pooled[key] = v if key not in pooled else jnp.maximum(pooled[key], v)
    stacked = jnp.concatenate(
        [pooled[z, y] for z in range(depth // 2) for y in range(height // 2)], axis=0
    )
    stacked = jnp.maximum(stacked, pltpu.roll(stacked, across - 1, 1)).astype(bf16)
    cells = (depth // 2) * (height // 2)
    size = cells * filters
    target = lax.broadcasted_iota(jnp.int32, (size, size), 0)
    source = lax.broadcasted_iota(jnp.int32, (size, size), 1)
    wanted = (target & (cells - 1)) * filters + target // cells
    rows_pick = jnp.where(source == wanted, 1.0, 0.0).astype(bf16)
    lane_from = lax.broadcasted_iota(jnp.int32, (across, across // 2), 0)
    lane_to = lax.broadcasted_iota(jnp.int32, (across, across // 2), 1)
    lanes_pick = jnp.where(lane_from == 2 * lane_to, 1.0, 0.0).astype(bf16)
    picked = jnp.dot(stacked, lanes_pick, preferred_element_type=f32).astype(bf16)
    out_ref[...] = jnp.dot(rows_pick, picked, preferred_element_type=f32).astype(bf16)


def gather(block, size):
    def swapped(x, r):
        pairs = [(i, i ^ (2 * r)) for i in range(size)]
        return lax.ppermute(x, "filt", pairs)

    far = size // 4
    held = {0: block}
    held[far] = swapped(block, far)
    for r in range(1, far):
        held[r] = swapped(block, r)
    for r in range(1, far):
        held[far ^ r] = swapped(held[far], r)
    return jnp.stack([held[r] for r in range(size // 2)])


def on_device(volume, kernel, filter_bias):
    block, depth, height, across = volume.shape
    filters, cin = kernel.shape[0], kernel.shape[-1]
    size = lax.axis_size("filt")
    count = lax.axis_size("space")
    here = lax.axis_index("space")
    place = lax.axis_index("filt")
    flags = jnp.stack([place & 1, place >> 1, here, count - 1 - here]).astype(jnp.int32)

    vmem = pl.BlockSpec(memory_space=pltpu.VMEM)
    smem = pl.BlockSpec(memory_space=pltpu.SMEM)
    shape = jax.ShapeDtypeStruct
    macs = 27 * filters * cin * depth * height * across
    padded = pltpu.VMEM((depth, cin // 2, (height + 2) * across), bf16)
    pairs = height // 2
    edges = 1 if count == 2 else 2

    def call(body, outs, ins, args, cost, scratch=()):
        return pl.pallas_call(
            body,
            out_shape=outs,
            in_specs=ins,
            out_specs=jax.tree.map(lambda _: vmem, outs),
            scratch_shapes=scratch,
            compiler_params=pltpu.CompilerParams(vmem_limit_bytes=16 << 20),
            cost_estimate=pl.CostEstimate(
                flops=int(cost * macs), bytes_accessed=1 << 20, transcendentals=0
            ),
        )(*args)

    blocks = volume.transpose(1, 2, 0, 3).reshape(depth * height, block, across)
    mine = gather(blocks, size)
    theirs = lax.ppermute(mine, "filt", [(i, i ^ 1) for i in range(size)])

    ordered = shape((9, 3 * filters, cin // 2), bf16)
    w_mine, w_theirs, bias = call(
        functools.partial(prepare, block=block),
        (ordered, ordered, shape((filters, across), f32)),
        [smem, vmem, vmem],
        (flags, kernel.transpose(1, 2, 3, 0, 4).reshape(-1, cin), filter_bias[None]),
        0.2,
    )
    dims = dict(depth=depth, height=height)
    partial, edge = call(
        functools.partial(first_half, count=count, **dims),
        (
            shape((depth * pairs, 3 * filters, 2 * across), f32),
            shape((edges * pairs, 3 * filters, 2 * across), f32),
        ),
        [smem, vmem, vmem],
        (flags, w_mine, mine),
        1.0,
        [padded],
    )
    sums = call(
        functools.partial(send_edges, count=count, **dims),
        shape((edges, height, filters, across), f32),
        [smem, vmem, vmem, vmem],
        (flags, w_theirs, theirs, edge),
        0.2,
    )
    if count == 2:
        got = [lax.ppermute(sums, "space", [(0, 1), (1, 0)])]
    else:
        up = [(i, i + 1) for i in range(count - 1)]
        down = [(t, s) for s, t in up]
        got = [lax.ppermute(sums[:1], "space", up), lax.ppermute(sums[1:], "space", down)]
    v = call(
        functools.partial(second_half, **dims),
        shape((depth * height, filters, across), f32),
        [vmem, vmem, vmem, vmem],
        (w_theirs, theirs, partial, bias),
        1.0,
        [padded],
    )
    pooled = call(
        functools.partial(finish, count=count, **dims),
        shape((filters * depth * height // 4, across // 2), bf16),
        [smem, vmem] + [vmem] * len(got),
        (flags, v, *got),
        0.2,
    )
    return pooled.reshape(filters, depth // 2, height // 2, across // 2)


def solution(mesh):
    in_specs = (P("filt", "space", None, None), P("filt", None, None, None, None), P("filt"))
    out_specs = P("filt", "space", None, None)
    return jax.shard_map(
        on_device, mesh=mesh, in_specs=in_specs, out_specs=out_specs, check_vma=False
    )
```

```python
import functools

import jax
import jax.numpy as jnp
from jax import lax
from jax.experimental import pallas as pl
from jax.experimental.pallas import tpu as pltpu
from jax.sharding import PartitionSpec as P

slope = 0.3
f32, bf16 = jnp.float32, jnp.bfloat16


def one_hot(shape, wanted):
    target = lax.broadcasted_iota(jnp.int32, shape, 0)
    source = lax.broadcasted_iota(jnp.int32, shape, 1)
    return jnp.where(source == wanted(target), 1.0, 0.0).astype(bf16)


def begin(flags_ref, vol_ref, own_ref, *plane_refs, count):
    depth = vol_ref.shape[1]
    own_ref[...] = vol_ref[...]
    if count == 2:
        plane_refs[0][...] = vol_ref[:, pl.ds(jnp.where(flags_ref[2] == 0, depth - 1, 0), 1)]
    else:
        plane_refs[0][...] = vol_ref[:, depth - 1 : depth]
        plane_refs[1][...] = vol_ref[:, 0:1]


def prepare(flags_ref, kernel_ref, bias_ref, w_mine_ref, w_theirs_ref, bias_out_ref, *, block):
    cin = kernel_ref.shape[-1]
    half = cin // 2
    far = half // block // 2
    core, group = flags_ref[0], flags_ref[1]
    source = lax.broadcasted_iota(jnp.int32, (cin, cin), 0)
    target = lax.broadcasted_iota(jnp.int32, (cin, cin), 1)
    place = target & (half - 1)
    part = jnp.where(target < half, core, 1 - core)
    slot = place // block
    relative = (slot >> 1) | ((slot & 1) * far)
    wanted = ((relative ^ group) * 2 + part) * block + (place & (block - 1))
    shuffle = jnp.where(source == wanted, 1.0, 0.0).astype(bf16)
    ordered = jnp.dot(kernel_ref[...], shuffle, preferred_element_type=f32).astype(bf16)
    w_mine_ref[...] = ordered[:, :half].reshape(w_mine_ref.shape)
    w_theirs_ref[...] = ordered[:, half:].reshape(w_theirs_ref.shape)
    filters = bias_ref.shape[1]
    row = lax.broadcasted_iota(jnp.int32, (filters, filters), 0)
    column = lax.broadcasted_iota(jnp.int32, (filters, filters), 1)
    spread = jnp.where(row == column, bias_ref[...].astype(f32), 0.0)
    bias_out_ref[...] = jnp.broadcast_to(
        jnp.sum(spread, axis=1, keepdims=True), bias_out_ref.shape
    )


def assemble(*refs, block, per_block):
    in_refs, out_ref = refs[:-2], refs[-1]
    parts = len(in_refs) // 2
    across = out_ref.shape[1]
    at = 0
    for k in range(parts):
        own, far = in_refs[k], in_refs[parts + k]
        rows = own.shape[0]
        cells = rows // block
        pick = one_hot((rows, rows), lambda t: (t & (block - 1)) * cells + t // block)
        both = jnp.concatenate([own[...], far[...]], axis=1)
        moved = jnp.dot(pick, both, preferred_element_type=f32).astype(bf16)
        out_ref[at : at + rows] = moved[:, :across]
        out_ref[per_block + at : per_block + at + rows] = moved[:, across:]
        at += rows


def rows_of(ref, row):
    return jnp.concatenate([ref[k, row] for k in range(ref.shape[0])], axis=0)


def fill_pad(flags_ref, vol_ref, pad_ref, depth, height):
    extra = vol_ref.shape[1] // height - depth
    for plane in range(depth + 2):
        if 1 <= plane <= depth:
            rows = [rows_of(vol_ref, (plane - 1) * height + y) for y in range(height)]
        else:
            which = 0 if plane == 0 or extra == 1 else 1
            rows = [rows_of(vol_ref, (depth + which) * height + y) for y in range(height)]
            keep = flags_ref[2 if plane == 0 else 3] > 0
            rows = [jnp.where(keep, r, jnp.zeros_like(r)) for r in rows]
        zero = jnp.zeros_like(rows[0])
        pad_ref[plane] = jnp.concatenate([zero] + rows + [zero], axis=1)


def product(w_ref, pad_ref, z, y, across):
    taps = [(a, b) for a in range(3) for b in range(3)]
    left = jnp.concatenate([w_ref[a * 3 + b] for a, b in taps], axis=1)
    right = jnp.concatenate(
        [pad_ref[z + a, :, (y + b) * across : (y + b + 2) * across] for a, b in taps], axis=0
    )
    return jnp.dot(left, right, preferred_element_type=f32)


def combine(total, k, filters, across):
    part = total[:, k * across : (k + 1) * across]
    lane = lax.broadcasted_iota(jnp.int32, (filters, across), 1)
    left = pltpu.roll(part[:filters], 1, 1)
    right = pltpu.roll(part[2 * filters :], across - 1, 1)
    v = part[filters : 2 * filters]
    v += jnp.where(lane > 0, left, 0.0)
    return v + jnp.where(lane < across - 1, right, 0.0)


def first_half(flags_ref, w_ref, vol_ref, sum_ref, pad_ref, *, depth, height):
    across = vol_ref.shape[-1]
    pairs = height // 2
    fill_pad(flags_ref, vol_ref, pad_ref, depth, height)
    for z in range(depth):
        for y in range(pairs):
            sum_ref[z * pairs + y] = product(w_ref, pad_ref, z, 2 * y, across)


def second_half(
    flags_ref, w_ref, vol_ref, sum_ref, bias_ref, out_ref, pad_ref, *, depth, height
):
    across = vol_ref.shape[-1]
    filters = bias_ref.shape[0]
    pairs = height // 2
    fill_pad(flags_ref, vol_ref, pad_ref, depth, height)
    pooled = {}
    for z in range(depth):
        for y in range(pairs):
            total = product(w_ref, pad_ref, z, 2 * y, across) + sum_ref[z * pairs + y]
            for j in range(2):
                v = combine(total, j, filters, across) + bias_ref[...]
                v = jnp.where(v > 0, v, slope * v)
                key = (z // 2, y)
                pooled[key] = v if key not in pooled else jnp.maximum(pooled[key], v)
    stacked = jnp.concatenate(
        [pooled[z, y] for z in range(depth // 2) for y in range(pairs)], axis=0
    )
    stacked = jnp.maximum(stacked, pltpu.roll(stacked, across - 1, 1)).astype(bf16)
    cells = (depth // 2) * pairs
    size = cells * filters
    rows_pick = one_hot((size, size), lambda t: (t & (cells - 1)) * filters + t // cells)
    lane_from = lax.broadcasted_iota(jnp.int32, (across, across // 2), 0)
    lane_to = lax.broadcasted_iota(jnp.int32, (across, across // 2), 1)
    lanes_pick = jnp.where(lane_from == 2 * lane_to, 1.0, 0.0).astype(bf16)
    picked = jnp.dot(stacked, lanes_pick, preferred_element_type=f32).astype(bf16)
    out_ref[...] = jnp.dot(rows_pick, picked, preferred_element_type=f32).astype(bf16)


def shifted(x, relative, step, size, count):
    pairs = []
    for f in range(size):
        for s in range(count):
            t = 1 - s if step == "swap" else s + step
            if 0 <= t < count:
                pairs.append((f * count + s, (f ^ (2 * relative)) * count + t))
    return lax.ppermute(x, ("filt", "space"), pairs)


def on_device(volume, kernel, filter_bias):
    block, depth, height, across = volume.shape
    filters, cin = kernel.shape[0], kernel.shape[-1]
    size = lax.axis_size("filt")
    count = lax.axis_size("space")
    here = lax.axis_index("space")
    place = lax.axis_index("filt")
    flags = jnp.stack([place & 1, place >> 1, here, count - 1 - here]).astype(jnp.int32)
    far = size // 4
    pairs = height // 2

    vmem = pl.BlockSpec(memory_space=pltpu.VMEM)
    smem = pl.BlockSpec(memory_space=pltpu.SMEM)
    shape = jax.ShapeDtypeStruct
    macs = 27 * filters * cin * depth * height * across
    padded = pltpu.VMEM((depth + 2, cin // 2, (height + 2) * across), bf16)

    def call(body, outs, ins, args, cost, scratch=()):
        return pl.pallas_call(
            body,
            out_shape=outs,
            in_specs=ins,
            out_specs=jax.tree.map(lambda _: vmem, outs),
            scratch_shapes=scratch,
            compiler_params=pltpu.CompilerParams(vmem_limit_bytes=16 << 20),
            cost_estimate=pl.CostEstimate(
                flops=int(cost * macs), bytes_accessed=1 << 20, transcendentals=0
            ),
        )(*args)

    far_block = shifted(volume, far, 0, size, count)
    plane = shape((block, 1, height, across), bf16)
    steps = ["swap"] if count == 2 else [1, -1]
    own_block, *edges = call(
        functools.partial(begin, count=count),
        [shape(volume.shape, bf16)] + [plane] * len(steps),
        [smem, vmem],
        (flags, volume),
        0.01,
    )
    sends = list(zip(edges, steps))
    own_planes = [shifted(x, 0, step, size, count) for x, step in sends]
    far_planes = [shifted(x, far, step, size, count) for x, step in sends]

    ordered = shape((9, 3 * filters, cin // 2), bf16)
    w_mine, w_theirs, bias = call(
        functools.partial(prepare, block=block),
        (ordered, ordered, shape((filters, across), f32)),
        [smem, vmem, vmem],
        (flags, kernel.transpose(1, 2, 3, 0, 4).reshape(-1, cin), filter_bias[None]),
        0.1,
    )

    rows = [x.reshape(-1, across) for x in [own_block] + own_planes + [far_block] + far_planes]
    cells = (depth + len(sends)) * height
    per_block = cells * block
    pair = call(
        functools.partial(assemble, block=block, per_block=per_block),
        shape((2 * per_block, across), bf16),
        [vmem] * len(rows) + [pl.BlockSpec(memory_space=pl.ANY)],
        rows + [w_mine],
        0.1,
    ).reshape(2, cells, block, across)
    near = [pair] + [shifted(pair, r, 0, size, count) for r in range(1, far)]
    mine = jnp.concatenate(near, axis=0)

    theirs = lax.ppermute(mine, "filt", [(i, i ^ 1) for i in range(size)])
    dims = dict(depth=depth, height=height)
    partial = call(
        functools.partial(first_half, **dims),
        shape((depth * pairs, 3 * filters, 2 * across), f32),
        [smem, vmem, vmem],
        (flags, w_mine, mine),
        8.0,
        [padded],
    )
    pooled = call(
        functools.partial(second_half, **dims),
        shape((filters * depth * height // 4, across // 2), bf16),
        [smem, vmem, vmem, vmem, vmem],
        (flags, w_theirs, theirs, partial, bias),
        1.0,
        [padded],
    )
    return pooled.reshape(filters, depth // 2, height // 2, across // 2)


def solution(mesh):
    in_specs = (P("filt", "space", None, None), P("filt", None, None, None, None), P("filt"))
    out_specs = P("filt", "space", None, None)
    return jax.shard_map(
        on_device, mesh=mesh, in_specs=in_specs, out_specs=out_specs, check_vma=False
    )
```

```python
import functools

import jax
import jax.numpy as jnp
from jax import lax
from jax.experimental import pallas as pl
from jax.experimental.pallas import tpu as pltpu
from jax.sharding import PartitionSpec as P

slope = 0.3
f32, bf16 = jnp.float32, jnp.bfloat16


def one_hot(shape, wanted):
    target = lax.broadcasted_iota(jnp.int32, shape, 0)
    source = lax.broadcasted_iota(jnp.int32, shape, 1)
    return jnp.where(source == wanted(target), 1.0, 0.0).astype(bf16)


def sort_rows(x, block):
    rows = x.shape[0]
    cells = rows // block
    pick = one_hot((rows, rows), lambda t: (t & (block - 1)) * cells + t // block)
    return jnp.dot(pick, x, preferred_element_type=f32).astype(bf16)


def begin(flags_ref, vol_ref, own_ref, *plane_refs, block, depth, count):
    own_ref[...] = sort_rows(vol_ref[...], block)
    rows = own_ref.shape[0] // depth
    if count == 2:
        at = jnp.where(flags_ref[2] == 0, (depth - 1) * rows, 0)
        plane_refs[0][...] = own_ref[pl.ds(pl.multiple_of(at, rows), rows)]
    else:
        plane_refs[0][...] = own_ref[(depth - 1) * rows :]
        plane_refs[1][...] = own_ref[:rows]


def prepare(flags_ref, kernel_ref, bias_ref, w_first_ref, w_last_ref, bias_out_ref, *, block):
    cin = kernel_ref.shape[-1]
    chunk, quarter = cin // 2, cin // 4
    far = chunk // block // 2
    core, group = flags_ref[0], flags_ref[1]
    source = lax.broadcasted_iota(jnp.int32, (cin, cin), 0)
    target = lax.broadcasted_iota(jnp.int32, (cin, cin), 1)
    part = jnp.where((target & quarter) == 0, core, 1 - core)
    place = target & (quarter - 1)
    slot = place // block
    near = (target // chunk) * (far // 2) + (slot >> 1)
    relative = near | ((slot & 1) * far)
    wanted = ((relative ^ group) * 2 + part) * block + (place & (block - 1))
    shuffle = jnp.where(source == wanted, 1.0, 0.0).astype(bf16)
    ordered = jnp.dot(kernel_ref[...], shuffle, preferred_element_type=f32).astype(bf16)
    w_first_ref[...] = ordered[:, :chunk].reshape(w_first_ref.shape)
    w_last_ref[...] = ordered[:, chunk:].reshape(w_last_ref.shape)
    filters = bias_ref.shape[1]
    row = lax.broadcasted_iota(jnp.int32, (filters, filters), 0)
    column = lax.broadcasted_iota(jnp.int32, (filters, filters), 1)
    spread = jnp.where(row == column, bias_ref[...].astype(f32), 0.0)
    bias_out_ref[...] = jnp.broadcast_to(
        jnp.sum(spread, axis=1, keepdims=True), bias_out_ref.shape
    )


def assemble(*refs, block):
    in_refs, pair_ref = refs[:-1], refs[-1]
    own_ref, far_ref = in_refs[0], in_refs[-1]
    size = own_ref.shape[0]
    at = size
    pair_ref[:size] = own_ref[...]
    for ref in in_refs[1:-1]:
        rows = ref.shape[0]
        pair_ref[at : at + rows] = ref[...]
        at += rows
    pair_ref[at:] = sort_rows(far_ref[...], block)


def join(*refs):
    in_refs, out_ref = refs[1:-1], refs[-1]
    at = 0
    for ref in in_refs:
        out_ref[at : at + ref.shape[0]] = ref[...]
        at += ref.shape[0]


def row_of(refs, plane, y, depth, height, extra):
    size, beside = depth * height, extra * height
    per_pair = 2 * (size + beside)
    pieces = []
    for ref in refs:
        for pair in range(ref.shape[0] // per_pair):
            for far in range(2):
                if 0 <= plane < depth:
                    at = far * (size + 2 * beside) + plane * height + y
                else:
                    which = 1 if plane == depth and extra == 2 else 0
                    at = size + far * beside + which * height + y
                pieces.append(ref[pair * per_pair + at])
    return jnp.concatenate(pieces, axis=0)


def products(flags_ref, w_ref, refs, depth, height, extra):
    zero = jnp.zeros((w_ref.shape[-1], refs[0].shape[-1]), bf16)
    weights = [w_ref[k] for k in range(9)]
    none = jnp.zeros_like(weights[0])
    for z in range(depth):
        left = []
        for a in range(3):
            for b in range(3):
                w = weights[a * 3 + b]
                if z + a - 1 < 0:
                    w = jnp.where(flags_ref[2] > 0, w, none)
                if z + a - 1 == depth:
                    w = jnp.where(flags_ref[3] > 0, w, none)
                left.append(w)
        left = jnp.concatenate(left, axis=1)
        rows = [
            [zero] + [row_of(refs, z + a - 1, y, depth, height, extra) for y in range(height)] + [zero]
            for a in range(3)
        ]
        for y in range(0, height, 2):
            right = jnp.concatenate(
                [
                    jnp.concatenate([rows[a][y + b], rows[a][y + b + 1]], axis=1)
                    for a in range(3)
                    for b in range(3)
                ],
                axis=0,
            )
            yield z, y, jnp.dot(left, right, preferred_element_type=f32)


def combine(total, k, filters, across):
    part = total[:, k * across : (k + 1) * across]
    lane = lax.broadcasted_iota(jnp.int32, (filters, across), 1)
    left = pltpu.roll(part[:filters], 1, 1)
    right = pltpu.roll(part[2 * filters :], across - 1, 1)
    v = part[filters : 2 * filters]
    v += jnp.where(lane > 0, left, 0.0)
    return v + jnp.where(lane < across - 1, right, 0.0)


def first_chunk(flags_ref, w_ref, mine_ref, theirs_ref, sum_ref, *, depth, height, extra):
    pairs = height // 2
    for z, y, total in products(flags_ref, w_ref, (mine_ref, theirs_ref), depth, height, extra):
        sum_ref[z * pairs + y // 2] = total


def last_chunk(
    flags_ref, w_ref, mine_ref, theirs_ref, sum_ref, bias_ref, out_ref, *, depth, height, extra
):
    across = mine_ref.shape[-1]
    filters = bias_ref.shape[0]
    pairs = height // 2
    pooled = {}
    for z, y, total in products(flags_ref, w_ref, (mine_ref, theirs_ref), depth, height, extra):
        total += sum_ref[z * pairs + y // 2]
        for j in range(2):
            v = combine(total, j, filters, across) + bias_ref[...]
            v = jnp.where(v > 0, v, slope * v)
            key = (z // 2, y // 2)
            pooled[key] = v if key not in pooled else jnp.maximum(pooled[key], v)
    stacked = jnp.concatenate(
        [pooled[z, y] for z in range(depth // 2) for y in range(pairs)], axis=0
    )
    stacked = jnp.maximum(stacked, pltpu.roll(stacked, across - 1, 1)).astype(bf16)
    cells = (depth // 2) * pairs
    size = cells * filters
    rows_pick = one_hot((size, size), lambda t: (t & (cells - 1)) * filters + t // cells)
    lane_from = lax.broadcasted_iota(jnp.int32, (across, across // 2), 0)
    lane_to = lax.broadcasted_iota(jnp.int32, (across, across // 2), 1)
    lanes_pick = jnp.where(lane_from == 2 * lane_to, 1.0, 0.0).astype(bf16)
    picked = jnp.dot(stacked, lanes_pick, preferred_element_type=f32).astype(bf16)
    out_ref[...] = jnp.dot(rows_pick, picked, preferred_element_type=f32).astype(bf16)


def shifted(x, relative, step, size, count):
    pairs = []
    for f in range(size):
        for s in range(count):
            t = 1 - s if step == "swap" else s + step
            if 0 <= t < count:
                pairs.append((f * count + s, (f ^ (2 * relative)) * count + t))
    return lax.ppermute(x, ("filt", "space"), pairs)


def on_device(volume, kernel, filter_bias):
    block, depth, height, across = volume.shape
    filters, cin = kernel.shape[0], kernel.shape[-1]
    size = lax.axis_size("filt")
    count = lax.axis_size("space")
    here = lax.axis_index("space")
    place = lax.axis_index("filt")
    flags = jnp.stack([place & 1, place >> 1, here, count - 1 - here]).astype(jnp.int32)
    far = size // 4
    pairs = height // 2

    vmem = pl.BlockSpec(memory_space=pltpu.VMEM)
    smem = pl.BlockSpec(memory_space=pltpu.SMEM)
    anywhere = pl.BlockSpec(memory_space=pl.ANY)
    shape = jax.ShapeDtypeStruct
    macs = 27 * filters * cin * depth * height * across

    def call(body, outs, ins, args, cost):
        return pl.pallas_call(
            body,
            out_shape=outs,
            in_specs=ins,
            out_specs=jax.tree.map(lambda _: vmem, outs),
            compiler_params=pltpu.CompilerParams(vmem_limit_bytes=16 << 20),
            cost_estimate=pl.CostEstimate(
                flops=int(cost * macs) >> 12, bytes_accessed=1 << 8, transcendentals=0
            ),
        )(*args)

    far_block = shifted(volume, far, 0, size, count)
    cells = depth * height * block
    beside = height * block
    steps = ["swap"] if count == 2 else [1, -1]
    extra = len(steps)
    own_block, *edges = call(
        functools.partial(begin, block=block, depth=depth, count=count),
        [shape((cells, across), bf16)] + [shape((beside, across), bf16)] * extra,
        [smem, vmem],
        (flags, volume.reshape(cells, across)),
        0.01,
    )
    sends = list(zip(edges, steps))
    far_planes = [shifted(x, far, step, size, count) for x, step in sends]
    own_planes = [shifted(x, 0, step, size, count) for x, step in sends]

    per_pair = 2 * (cells + extra * beside)
    pair = call(
        functools.partial(assemble, block=block),
        shape((per_pair, across), bf16),
        [vmem] * (2 + 2 * extra),
        [own_block] + own_planes + far_planes + [far_block.reshape(cells, across)],
        0.05,
    )
    near = [pair] + [shifted(pair, r, 0, size, count) for r in range(1, far)]

    ordered = shape((9, 3 * filters, cin // 2), bf16)
    w_first, w_last, bias = call(
        functools.partial(prepare, block=block),
        (ordered, ordered, shape((filters, across), f32)),
        [smem, vmem, vmem],
        (flags, kernel.transpose(1, 2, 3, 0, 4).reshape(-1, cin), filter_bias[None]),
        0.1,
    )

    def both_cores(parts):
        mine = call(
            join,
            shape((far // 2 * per_pair, across), bf16),
            [anywhere] + [vmem] * len(parts),
            [w_first] + parts,
            0.05,
        ).reshape(-1, block, across)
        return mine, lax.ppermute(mine, "filt", [(i, i ^ 1) for i in range(size)])

    dims = dict(depth=depth, height=height, extra=extra)
    mine, theirs = both_cores(near[: far // 2])
    partial = call(
        functools.partial(first_chunk, **dims),
        shape((depth * pairs, 3 * filters, 2 * across), f32),
        [smem, vmem, vmem, vmem],
        (flags, w_first, mine, theirs),
        4.0,
    )
    mine, theirs = both_cores(near[far // 2 :])
    pooled = call(
        functools.partial(last_chunk, **dims),
        shape((filters * depth * height // 4, across // 2), bf16),
        [smem, vmem, vmem, vmem, vmem, vmem],
        (flags, w_last, mine, theirs, partial, bias),
        1.0,
    )
    return pooled.reshape(filters, depth // 2, height // 2, across // 2)


def solution(mesh):
    in_specs = (P("filt", "space", None, None), P("filt", None, None, None, None), P("filt"))
    out_specs = P("filt", "space", None, None)
    return jax.shard_map(
        on_device, mesh=mesh, in_specs=in_specs, out_specs=out_specs, check_vma=False
    )
```

```python
import functools

import jax
import jax.numpy as jnp
from jax import lax
from jax.experimental import pallas as pl
from jax.experimental.pallas import tpu as pltpu
from jax.sharding import PartitionSpec as P

slope = 0.3
f32, bf16 = jnp.float32, jnp.bfloat16


def one_hot(shape, wanted):
    target = lax.broadcasted_iota(jnp.int32, shape, 0)
    source = lax.broadcasted_iota(jnp.int32, shape, 1)
    return jnp.where(source == wanted(target), 1.0, 0.0).astype(bf16)


def sort_rows(x, block):
    rows = x.shape[0]
    cells = rows // block
    pick = one_hot((rows, rows), lambda t: (t & (block - 1)) * cells + t // block)
    return jnp.dot(pick, x, preferred_element_type=f32).astype(bf16)


def begin(flags_ref, vol_ref, kernel_ref, bias_ref, own_ref, *refs, block, depth, count):
    plane_refs, (w_ref, bias_out_ref, raw_ref, done) = refs[:-4], refs[-4:]
    copies = [
        pltpu.make_async_copy(source, target, done.at[k])
        for k, (source, target) in enumerate(
            [(vol_ref, raw_ref), (kernel_ref, w_ref), (bias_ref, bias_out_ref)]
        )
    ]
    for copy in copies:
        copy.start()
    copies[0].wait()
    own_ref[...] = sort_rows(raw_ref[...], block)
    rows = own_ref.shape[0] // depth
    if count == 2:
        at = jnp.where(flags_ref[2] == 0, (depth - 1) * rows, 0)
        plane_refs[0][...] = own_ref[pl.ds(pl.multiple_of(at, rows), rows)]
    else:
        plane_refs[0][...] = own_ref[(depth - 1) * rows :]
        plane_refs[1][...] = own_ref[:rows]
    for copy in copies[1:]:
        copy.wait()


def prepare(flags_ref, kernel_ref, bias_ref, w_mine_ref, w_theirs_ref, bias_out_ref, *, block):
    cin = kernel_ref.shape[-1]
    half = cin // 2
    far = half // block // 2
    shift = block.bit_length() - 1
    core, group = flags_ref[0], flags_ref[1]
    source = lax.broadcasted_iota(jnp.int32, (cin, cin), 0)
    target = lax.broadcasted_iota(jnp.int32, (1, cin), 1)
    part = jnp.where(target < half, core, 1 - core)
    slot = (target & (half - 1)) >> shift
    relative = (slot >> 1) | jnp.where((slot & 1) > 0, far, 0)
    wanted = ((((relative ^ group) << 1) | part) << shift) | (target & (block - 1))
    shuffle = jnp.where(source == wanted, 1.0, 0.0).astype(bf16)
    ordered = jnp.dot(kernel_ref[...], shuffle, preferred_element_type=f32).astype(bf16)
    w_mine_ref[...] = ordered[:, :half].reshape(w_mine_ref.shape)
    w_theirs_ref[...] = ordered[:, half:].reshape(w_theirs_ref.shape)
    filters = bias_ref.shape[1]
    row = lax.broadcasted_iota(jnp.int32, (filters, filters), 0)
    column = lax.broadcasted_iota(jnp.int32, (filters, filters), 1)
    spread = jnp.where(row == column, bias_ref[...].astype(f32), 0.0)
    bias_out_ref[...] = jnp.broadcast_to(
        jnp.sum(spread, axis=1, keepdims=True), bias_out_ref.shape
    )


def assemble(_, own_ref, far_ref, pair_ref, *, block):
    size = own_ref.shape[0]
    pair_ref[:size] = own_ref[...]
    pair_ref[size:] = sort_rows(far_ref[...], block)


def join(*refs):
    in_refs, out_ref = refs[1:-1], refs[-1]
    at = 0
    for ref in in_refs:
        out_ref[at : at + ref.shape[0]] = ref[...]
        at += ref.shape[0]


def channels(refs, per_block, row):
    return jnp.concatenate(
        [ref[k * per_block + row] for ref in refs for k in range(ref.shape[0] // per_block)],
        axis=0,
    )


def windows(rows):
    zero = jnp.zeros_like(rows[0])
    rows = [zero] + rows + [zero]
    return [
        [jnp.concatenate([rows[y + b], rows[y + b + 1]], axis=1) for b in range(3)]
        for y in range(0, len(rows) - 2, 2)
    ]


def products(w_ref, refs, depth, height):
    cells = depth * height
    for z in range(depth):
        taps = [a for a in range(3) if 0 <= z + a - 1 < depth]
        left = jnp.concatenate([w_ref[a * 3 + b] for a in taps for b in range(3)], axis=1)
        views = [
            windows([channels(refs, cells, (z + a - 1) * height + y) for y in range(height)])
            for a in taps
        ]
        for y in range(height // 2):
            right = jnp.concatenate([w for view in views for w in view[y]], axis=0)
            yield z, y, jnp.dot(left, right, preferred_element_type=f32)


def combine(total, k, filters, across):
    part = total[:, k * across : (k + 1) * across]
    lane = lax.broadcasted_iota(jnp.int32, (filters, across), 1)
    left = pltpu.roll(part[:filters], 1, 1)
    right = pltpu.roll(part[2 * filters :], across - 1, 1)
    v = part[filters : 2 * filters]
    v += jnp.where(lane > 0, left, 0.0)
    return v + jnp.where(lane < across - 1, right, 0.0)


def own_parity(w_ref, *refs, depth, height):
    refs, sum_ref = refs[:-1], refs[-1]
    for z, y, total in products(w_ref, refs, depth, height):
        sum_ref[z * (height // 2) + y] = total


def other_parity(w_ref, bias_ref, sum_ref, *refs, depth, height):
    refs, v_ref = refs[:-1], refs[-1]
    filters, across = bias_ref.shape
    for z, y, total in products(w_ref, refs, depth, height):
        total += sum_ref[z * (height // 2) + y]
        for j in range(2):
            v_ref[z * height + 2 * y + j] = combine(total, j, filters, across) + bias_ref[...]


def finish(flags_ref, w_mine_ref, w_theirs_ref, v_ref, *refs, depth, height, count):
    refs, out_ref = refs[:-1], refs[-1]
    filters, across = v_ref.shape[1:]
    extra = 1 if count == 2 else 2
    beside = []
    for which in range(extra):
        tap = 2 * which if extra == 2 else jnp.where(flags_ref[2] > 0, 0, 2)
        left = jnp.concatenate(
            [w[tap * 3 + b] for b in range(3) for w in (w_mine_ref, w_theirs_ref)], axis=1
        )
        rows = [channels(refs, extra * height, which * height + y) for y in range(height)]
        added = []
        for view in windows(rows):
            total = jnp.dot(left, jnp.concatenate(view, axis=0), preferred_element_type=f32)
            added += [combine(total, j, filters, across) for j in range(2)]
        beside.append(added)
    pooled = {}
    for z in range(depth):
        for y in range(height):
            v = v_ref[z * height + y]
            if z == 0:
                v += jnp.where(flags_ref[2] > 0, beside[0][y], 0.0)
            if z == depth - 1:
                v += jnp.where(flags_ref[3] > 0, beside[-1][y], 0.0)
            v = jnp.where(v > 0, v, slope * v)
            key = (z // 2, y // 2)
            pooled[key] = v if key not in pooled else jnp.maximum(pooled[key], v)
    stacked = jnp.concatenate(
        [pooled[z, y] for z in range(depth // 2) for y in range(height // 2)], axis=0
    )
    stacked = jnp.maximum(stacked, pltpu.roll(stacked, across - 1, 1)).astype(bf16)
    cells = (depth // 2) * (height // 2)
    size = cells * filters
    rows_pick = one_hot((size, size), lambda t: (t & (cells - 1)) * filters + t // cells)
    lane_from = lax.broadcasted_iota(jnp.int32, (across, across // 2), 0)
    lane_to = lax.broadcasted_iota(jnp.int32, (across, across // 2), 1)
    lanes_pick = jnp.where(lane_from == 2 * lane_to, 1.0, 0.0).astype(bf16)
    picked = jnp.dot(stacked, lanes_pick, preferred_element_type=f32).astype(bf16)
    out_ref[...] = jnp.dot(rows_pick, picked, preferred_element_type=f32).astype(bf16)


def shifted(x, relative, step, size, count):
    pairs = []
    for f in range(size):
        for s in range(count):
            t = 1 - s if step == "swap" else s + step
            if 0 <= t < count:
                pairs.append((f * count + s, (f ^ (2 * relative)) * count + t))
    return lax.ppermute(x, ("filt", "space"), pairs)


def on_device(volume, kernel, filter_bias):
    block, depth, height, across = volume.shape
    filters, cin = kernel.shape[0], kernel.shape[-1]
    size = lax.axis_size("filt")
    count = lax.axis_size("space")
    here = lax.axis_index("space")
    place = lax.axis_index("filt")
    flags = jnp.stack([place & 1, place >> 1, here, count - 1 - here]).astype(jnp.int32)
    far = size // 4
    pairs = height // 2
    cells = depth * height * block
    beside = height * block
    steps = ["swap"] if count == 2 else [1, -1]
    extra = len(steps)

    vmem = pl.BlockSpec(memory_space=pltpu.VMEM)
    smem = pl.BlockSpec(memory_space=pltpu.SMEM)
    hbm = pl.BlockSpec(memory_space=pltpu.HBM)
    anywhere = pl.BlockSpec(memory_space=pl.ANY)
    shape = jax.ShapeDtypeStruct

    def call(body, outs, ins, args, scratch=(), cost=12):
        return pl.pallas_call(
            body,
            out_shape=outs,
            in_specs=ins,
            out_specs=jax.tree.map(lambda _: vmem, outs),
            scratch_shapes=scratch,
            compiler_params=pltpu.CompilerParams(vmem_limit_bytes=16 << 20),
            cost_estimate=pl.CostEstimate(flops=1 << cost, bytes_accessed=1 << 8, transcendentals=0),
        )(*args)

    far_block = shifted(volume, far, 0, size, count)
    weights = kernel.transpose(1, 2, 3, 0, 4).reshape(-1, cin)
    given = [volume.reshape(cells, across), weights, filter_bias[None]]
    own_block, *edges, weights, bias = call(
        functools.partial(begin, block=block, depth=depth, count=count),
        [shape((cells, across), bf16)]
        + [shape((beside, across), bf16)] * extra
        + [shape(weights.shape, bf16), shape((1, filters), bf16)],
        [smem, hbm, hbm, hbm],
        [flags] + [pltpu.with_memory_space_constraint(x, pltpu.HBM) for x in given],
        [pltpu.VMEM((cells, across), bf16), pltpu.SemaphoreType.DMA((3,))],
    )
    sends = list(zip(edges, steps))
    far_planes = [shifted(x, far, step, size, count) for x, step in sends]
    own_planes = [shifted(x, 0, step, size, count) for x, step in sends]
    ordered = shape((9, 3 * filters, cin // 2), bf16)
    w_mine, w_theirs, bias = call(
        functools.partial(prepare, block=block),
        (ordered, ordered, shape((filters, across), f32)),
        [smem, vmem, vmem],
        (flags, weights, bias),
        cost=31,
    )

    pair = call(
        functools.partial(assemble, block=block),
        shape((2 * cells, across), bf16),
        [anywhere, vmem, vmem],
        (w_mine, own_block, far_block.reshape(cells, across)),
        cost=31,
    )
    planes = call(
        join,
        shape((2 * extra * beside, across), bf16),
        [anywhere] + [vmem] * (2 * extra),
        [pair] + own_planes + far_planes,
        cost=31,
    )

    def near(x):
        parts = [x] + [shifted(x, r, 0, size, count) for r in range(1, far)]
        return [part.reshape(-1, block, across) for part in parts]

    def swapped(x):
        return lax.ppermute(x, "filt", [(i, i ^ 1) for i in range(size)])

    mine = near(pair)
    theirs = [swapped(jnp.concatenate(mine[k : k + far // 2], axis=0)) for k in (0, far // 2)]
    dims = dict(depth=depth, height=height)
    partial = call(
        functools.partial(own_parity, **dims),
        shape((depth * pairs, 3 * filters, 2 * across), f32),
        [vmem] * (1 + far),
        [w_mine] + mine,
        cost=28,
    )
    again = call(join, shape(planes.shape, bf16), [anywhere, vmem], (mine[1], planes), cost=12)
    behind = [shifted(planes, r, 0, size, count) for r in range(2, far)]
    behind = [planes, shifted(again, 1, 0, size, count)] + behind
    planes = call(
        join,
        shape((far * planes.shape[0], across), bf16),
        [anywhere] + [vmem] * far,
        [partial] + behind,
    ).reshape(-1, block, across)
    v = call(
        functools.partial(other_parity, **dims),
        shape((depth * height, filters, across), f32),
        [vmem] * 5,
        [w_theirs, bias, partial] + theirs,
    )
    pooled = call(
        functools.partial(finish, count=count, **dims),
        shape((filters * depth * height // 4, across // 2), bf16),
        [smem] + [vmem] * 5,
        (flags, w_mine, w_theirs, v, planes, swapped(planes)),
    )
    return pooled.reshape(filters, depth // 2, height // 2, across // 2)


def solution(mesh):
    in_specs = (P("filt", "space", None, None), P("filt", None, None, None, None), P("filt"))
    out_specs = P("filt", "space", None, None)
    return jax.shard_map(
        on_device, mesh=mesh, in_specs=in_specs, out_specs=out_specs, check_vma=False
    )
```

```python
import functools

import jax
import jax.numpy as jnp
from jax import lax
from jax.experimental import pallas as pl
from jax.experimental.pallas import tpu as pltpu
from jax.sharding import PartitionSpec as P

slope = 0.3
f32, bf16 = jnp.float32, jnp.bfloat16


def one_hot(shape, wanted):
    target = lax.broadcasted_iota(jnp.int32, shape, 0)
    source = lax.broadcasted_iota(jnp.int32, shape, 1)
    return jnp.where(source == wanted(target), 1.0, 0.0).astype(bf16)


def sort_rows(x, block):
    rows = x.shape[0]
    cells = rows // block
    pick = one_hot((rows, rows), lambda t: (t & (block - 1)) * cells + t // block)
    return jnp.dot(pick, x, preferred_element_type=f32).astype(bf16)


def begin(flags_ref, vol_ref, kernel_ref, bias_ref, own_ref, *refs, block, depth, count):
    plane_refs, (w_ref, bias_out_ref, raw_ref, done) = refs[:-4], refs[-4:]
    copies = [
        pltpu.make_async_copy(source, target, done.at[k])
        for k, (source, target) in enumerate(
            [(vol_ref, raw_ref), (kernel_ref, w_ref), (bias_ref, bias_out_ref)]
        )
    ]
    for copy in copies:
        copy.start()
    copies[0].wait()
    own_ref[...] = sort_rows(raw_ref[...], block)
    rows = own_ref.shape[0] // depth
    if count == 2:
        at = jnp.where(flags_ref[2] == 0, (depth - 1) * rows, 0)
        plane_refs[0][...] = own_ref[pl.ds(pl.multiple_of(at, rows), rows)]
    else:
        plane_refs[0][...] = own_ref[(depth - 1) * rows :]
        plane_refs[1][...] = own_ref[:rows]
    for copy in copies[1:]:
        copy.wait()


def prepare(flags_ref, kernel_ref, bias_ref, w_mine_ref, w_theirs_ref, bias_out_ref, *, block):
    cin = kernel_ref.shape[-1]
    half = cin // 2
    far = half // block // 2
    shift = block.bit_length() - 1
    core, group = flags_ref[0], flags_ref[1]
    source = lax.broadcasted_iota(jnp.int32, (cin, cin), 0)
    target = lax.broadcasted_iota(jnp.int32, (1, cin), 1)
    part = jnp.where(target < half, core, 1 - core)
    slot = (target & (half - 1)) >> shift
    relative = (slot >> 1) | jnp.where((slot & 1) > 0, far, 0)
    wanted = ((((relative ^ group) << 1) | part) << shift) | (target & (block - 1))
    shuffle = jnp.where(source == wanted, 1.0, 0.0).astype(bf16)
    ordered = jnp.dot(kernel_ref[...], shuffle, preferred_element_type=f32).astype(bf16)
    w_mine_ref[...] = ordered[:, :half].reshape(w_mine_ref.shape)
    w_theirs_ref[...] = ordered[:, half:].reshape(w_theirs_ref.shape)
    filters = bias_ref.shape[1]
    row = lax.broadcasted_iota(jnp.int32, (filters, filters), 0)
    column = lax.broadcasted_iota(jnp.int32, (filters, filters), 1)
    spread = jnp.where(row == column, bias_ref[...].astype(f32), 0.0)
    bias_out_ref[...] = jnp.broadcast_to(
        jnp.sum(spread, axis=1, keepdims=True), bias_out_ref.shape
    )


def assemble(_, own_ref, far_ref, pair_ref, *, block):
    size = own_ref.shape[0]
    pair_ref[:size] = own_ref[...]
    pair_ref[size:] = sort_rows(far_ref[...], block)


def join(*refs):
    in_refs, out_ref = refs[1:-1], refs[-1]
    at = 0
    for ref in in_refs:
        out_ref[at : at + ref.shape[0]] = ref[...]
        at += ref.shape[0]


def channels(refs, per_block, row):
    return jnp.concatenate(
        [ref[k * per_block + row] for ref in refs for k in range(ref.shape[0] // per_block)],
        axis=0,
    )


def windows(rows):
    zero = jnp.zeros_like(rows[0])
    rows = [zero] + rows + [zero]
    return [
        [jnp.concatenate([rows[y + b], rows[y + b + 1]], axis=1) for b in range(3)]
        for y in range(0, len(rows) - 2, 2)
    ]


def products(w_ref, refs, depth, height):
    cells = depth * height
    for z in range(depth):
        taps = [a for a in range(3) if 0 <= z + a - 1 < depth]
        left = jnp.concatenate([w_ref[a * 3 + b] for a in taps for b in range(3)], axis=1)
        views = [
            windows([channels(refs, cells, (z + a - 1) * height + y) for y in range(height)])
            for a in taps
        ]
        for y in range(height // 2):
            right = jnp.concatenate([w for view in views for w in view[y]], axis=0)
            yield z, y, jnp.dot(left, right, preferred_element_type=f32)


def combine(total, k, filters, across):
    part = total[:, k * across : (k + 1) * across]
    lane = lax.broadcasted_iota(jnp.int32, (filters, across), 1)
    left = pltpu.roll(part[:filters], 1, 1)
    right = pltpu.roll(part[2 * filters :], across - 1, 1)
    v = part[filters : 2 * filters]
    v += jnp.where(lane > 0, left, 0.0)
    return v + jnp.where(lane < across - 1, right, 0.0)


def own_parity(w_ref, *refs, depth, height):
    refs, sum_ref = refs[:-1], refs[-1]
    for z, y, total in products(w_ref, refs, depth, height):
        sum_ref[z * (height // 2) + y] = total


def other_parity(w_ref, bias_ref, sum_ref, *refs, depth, height):
    refs, v_ref = refs[:-1], refs[-1]
    filters, across = bias_ref.shape
    for z, y, total in products(w_ref, refs, depth, height):
        total += sum_ref[z * (height // 2) + y]
        for j in range(2):
            v_ref[z * height + 2 * y + j] = combine(total, j, filters, across) + bias_ref[...]


def finish(flags_ref, w_mine_ref, w_theirs_ref, v_ref, *refs, depth, height, count):
    refs, out_ref = refs[:-1], refs[-1]
    filters, across = v_ref.shape[1:]
    extra = 1 if count == 2 else 2
    beside = []
    for which in range(extra):
        tap = 2 * which if extra == 2 else jnp.where(flags_ref[2] > 0, 0, 2)
        left = jnp.concatenate(
            [w[tap * 3 + b] for b in range(3) for w in (w_mine_ref, w_theirs_ref)], axis=1
        )
        rows = [channels(refs, extra * height, which * height + y) for y in range(height)]
        added = []
        for view in windows(rows):
            total = jnp.dot(left, jnp.concatenate(view, axis=0), preferred_element_type=f32)
            added += [combine(total, j, filters, across) for j in range(2)]
        beside.append(added)
    pooled = {}
    for z in range(depth):
        for y in range(height):
            v = v_ref[z * height + y]
            if z == 0:
                v += jnp.where(flags_ref[2] > 0, beside[0][y], 0.0)
            if z == depth - 1:
                v += jnp.where(flags_ref[3] > 0, beside[-1][y], 0.0)
            v = jnp.where(v > 0, v, slope * v)
            key = (z // 2, y // 2)
            pooled[key] = v if key not in pooled else jnp.maximum(pooled[key], v)
    stacked = jnp.concatenate(
        [pooled[z, y] for z in range(depth // 2) for y in range(height // 2)], axis=0
    )
    stacked = jnp.maximum(stacked, pltpu.roll(stacked, across - 1, 1)).astype(bf16)
    cells = (depth // 2) * (height // 2)
    size = cells * filters
    rows_pick = one_hot((size, size), lambda t: (t & (cells - 1)) * filters + t // cells)
    lane_from = lax.broadcasted_iota(jnp.int32, (across, across // 2), 0)
    lane_to = lax.broadcasted_iota(jnp.int32, (across, across // 2), 1)
    lanes_pick = jnp.where(lane_from == 2 * lane_to, 1.0, 0.0).astype(bf16)
    picked = jnp.dot(stacked, lanes_pick, preferred_element_type=f32).astype(bf16)
    out_ref[...] = jnp.dot(rows_pick, picked, preferred_element_type=f32).astype(bf16)


def shifted(x, relative, step, size, count):
    pairs = []
    for f in range(size):
        for s in range(count):
            t = 1 - s if step == "swap" else s + step
            if 0 <= t < count:
                pairs.append((f * count + s, (f ^ (2 * relative)) * count + t))
    return lax.ppermute(x, ("filt", "space"), pairs)


def on_device(volume, kernel, filter_bias):
    block, depth, height, across = volume.shape
    filters, cin = kernel.shape[0], kernel.shape[-1]
    size = lax.axis_size("filt")
    count = lax.axis_size("space")
    here = lax.axis_index("space")
    place = lax.axis_index("filt")
    flags = jnp.stack([place & 1, place >> 1, here, count - 1 - here]).astype(jnp.int32)
    far = size // 4
    pairs = height // 2
    cells = depth * height * block
    beside = height * block
    steps = ["swap"] if count == 2 else [1, -1]
    extra = len(steps)

    vmem = pl.BlockSpec(memory_space=pltpu.VMEM)
    smem = pl.BlockSpec(memory_space=pltpu.SMEM)
    hbm = pl.BlockSpec(memory_space=pltpu.HBM)
    anywhere = pl.BlockSpec(memory_space=pl.ANY)
    shape = jax.ShapeDtypeStruct

    def call(body, outs, ins, args, scratch=(), cost=12):
        return pl.pallas_call(
            body,
            out_shape=outs,
            in_specs=ins,
            out_specs=jax.tree.map(lambda _: vmem, outs),
            scratch_shapes=scratch,
            compiler_params=pltpu.CompilerParams(vmem_limit_bytes=16 << 20),
            cost_estimate=pl.CostEstimate(flops=1 << cost, bytes_accessed=1 << 8, transcendentals=0),
        )(*args)

    far_block = shifted(volume, far, 0, size, count)
    weights = kernel.transpose(1, 2, 3, 0, 4).reshape(-1, cin)
    given = [volume.reshape(cells, across), weights, filter_bias[None]]
    own_block, *edges, weights, bias = call(
        functools.partial(begin, block=block, depth=depth, count=count),
        [shape((cells, across), bf16)]
        + [shape((beside, across), bf16)] * extra
        + [shape(weights.shape, bf16), shape((1, filters), bf16)],
        [smem, hbm, hbm, hbm],
        [flags] + [pltpu.with_memory_space_constraint(x, pltpu.HBM) for x in given],
        [pltpu.VMEM((cells, across), bf16), pltpu.SemaphoreType.DMA((3,))],
    )
    sends = list(zip(edges, steps))
    far_planes = [shifted(x, far, step, size, count) for x, step in sends]
    own_planes = [shifted(x, 0, step, size, count) for x, step in sends]
    ordered = shape((9, 3 * filters, cin // 2), bf16)
    w_mine, w_theirs, bias = call(
        functools.partial(prepare, block=block),
        (ordered, ordered, shape((filters, across), f32)),
        [smem, vmem, vmem],
        (flags, weights, bias),
        cost=31,
    )

    pair = call(
        functools.partial(assemble, block=block),
        shape((2 * cells, across), bf16),
        [anywhere, vmem, vmem],
        (w_mine, own_block, far_block.reshape(cells, across)),
        cost=31,
    )
    planes = call(
        join,
        shape((2 * extra * beside, across), bf16),
        [anywhere] + [vmem] * (2 * extra),
        [pair] + own_planes + far_planes,
        cost=31,
    )

    def near(x):
        parts = [x] + [shifted(x, r, 0, size, count) for r in range(1, far)]
        return [part.reshape(-1, block, across) for part in parts]

    def swapped(x):
        return lax.ppermute(x, "filt", [(i, i ^ 1) for i in range(size)])

    mine = near(pair)
    theirs = [swapped(x) for x in mine]
    dims = dict(depth=depth, height=height)
    partial = call(
        functools.partial(own_parity, **dims),
        shape((depth * pairs, 3 * filters, 2 * across), f32),
        [vmem] * (1 + far),
        [w_mine] + mine,
        cost=28,
    )
    again = call(join, shape(planes.shape, bf16), [anywhere, vmem], (mine[1], planes), cost=12)
    behind = [shifted(planes, r, 0, size, count) for r in range(2, far)]
    behind = [planes, shifted(again, 1, 0, size, count)] + behind
    planes = call(
        join,
        shape((far * planes.shape[0], across), bf16),
        [anywhere] + [vmem] * far,
        [partial] + behind,
    ).reshape(-1, block, across)
    v = call(
        functools.partial(other_parity, **dims),
        shape((depth * height, filters, across), f32),
        [vmem] * (3 + far),
        [w_theirs, bias, partial] + theirs,
    )
    pooled = call(
        functools.partial(finish, count=count, **dims),
        shape((filters * depth * height // 4, across // 2), bf16),
        [smem] + [vmem] * 5,
        (flags, w_mine, w_theirs, v, planes, swapped(planes)),
    )
    return pooled.reshape(filters, depth // 2, height // 2, across // 2)


def solution(mesh):
    in_specs = (P("filt", "space", None, None), P("filt", None, None, None, None), P("filt"))
    out_specs = P("filt", "space", None, None)
    return jax.shard_map(
        on_device, mesh=mesh, in_specs=in_specs, out_specs=out_specs, check_vma=False
    )
```

```python
import functools

import jax
import jax.numpy as jnp
from jax import lax
from jax.experimental import pallas as pl
from jax.experimental.pallas import tpu as pltpu
from jax.sharding import PartitionSpec as P

slope = 0.3
f32, bf16 = jnp.float32, jnp.bfloat16


def one_hot(shape, wanted):
    target = lax.broadcasted_iota(jnp.int32, (shape[0], 1), 0)
    source = lax.broadcasted_iota(jnp.int32, shape, 1)
    return jnp.where(source == wanted(target), 1.0, 0.0).astype(bf16)


def pick_rows(x, block, count, first):
    rows = x.shape[0]
    cells = rows // block
    shift = block.bit_length() - 1
    pick = one_hot(
        (count * block, rows), lambda t: (t & (block - 1)) * cells + (t >> shift) + first
    )
    return jnp.dot(pick, x, preferred_element_type=f32).astype(bf16)


def begin(flags_ref, vol_ref, kernel_ref, bias_ref, own_ref, *refs, block, depth, count):
    plane_refs, (w_ref, bias_out_ref, done) = refs[:-3], refs[-3:]
    copies = [
        pltpu.make_async_copy(source, target, done.at[k])
        for k, (source, target) in enumerate(
            [(vol_ref, own_ref), (kernel_ref, w_ref), (bias_ref, bias_out_ref)]
        )
    ]
    for copy in copies:
        copy.start()
    height = own_ref.shape[0] // block // depth
    last = (depth - 1) * height
    copies[0].wait()
    if count == 2:
        firsts = [jnp.where(flags_ref[2] == 0, last, 0)]
    else:
        firsts = [last, 0]
    for ref, first in zip(plane_refs, firsts):
        ref[...] = pick_rows(own_ref[...], block, height, first)
    for copy in copies[1:]:
        copy.wait()


def prepare(flags_ref, _, kernel_ref, bias_ref, w_mine_ref, w_theirs_ref, bias_out_ref, *, block):
    cin = kernel_ref.shape[-1]
    half = cin // 2
    far = half // block // 2
    shift = block.bit_length() - 1
    core, group = flags_ref[0], flags_ref[1]
    source = lax.broadcasted_iota(jnp.int32, (cin, cin), 0)
    target = lax.broadcasted_iota(jnp.int32, (1, cin), 1)
    part = jnp.where(target < half, core, 1 - core)
    slot = (target & (half - 1)) >> shift
    relative = (slot >> 1) | jnp.where((slot & 1) > 0, far, 0)
    wanted = ((((relative ^ group) << 1) | part) << shift) | (target & (block - 1))
    shuffle = jnp.where(source == wanted, 1.0, 0.0).astype(bf16)
    ordered = jnp.dot(kernel_ref[...], shuffle, preferred_element_type=f32).astype(bf16)
    w_mine_ref[...] = ordered[:, :half].reshape(w_mine_ref.shape)
    w_theirs_ref[...] = ordered[:, half:].reshape(w_theirs_ref.shape)
    filters = bias_ref.shape[1]
    row = lax.broadcasted_iota(jnp.int32, (filters, filters), 0)
    column = lax.broadcasted_iota(jnp.int32, (filters, filters), 1)
    spread = jnp.where(row == column, bias_ref[...].astype(f32), 0.0)
    bias_out_ref[...] = jnp.broadcast_to(
        jnp.sum(spread, axis=1, keepdims=True), bias_out_ref.shape
    )


def assemble(own_ref, far_ref, pair_ref, *, block):
    size, across = own_ref.shape
    both = jnp.concatenate([own_ref[...], far_ref[...]], axis=1)
    moved = pick_rows(both, block, size // block, 0)
    pair_ref[:size] = moved[:, :across]
    pair_ref[size:] = moved[:, across:]


def join(*refs):
    in_refs, out_ref = refs[1:-1], refs[-1]
    at = 0
    for ref in in_refs:
        out_ref[at : at + ref.shape[0]] = ref[...]
        at += ref.shape[0]


def channels(refs, per_block, row):
    return jnp.concatenate(
        [ref[k * per_block + row] for ref in refs for k in range(ref.shape[0] // per_block)],
        axis=0,
    )


def windows(rows):
    zero = jnp.zeros_like(rows[0])
    rows = [zero] + rows + [zero]
    return [
        [jnp.concatenate([rows[y + b], rows[y + b + 1]], axis=1) for b in range(3)]
        for y in range(0, len(rows) - 2, 2)
    ]


def products(w_ref, refs, depth, height):
    cells = depth * height
    for z in range(depth):
        taps = [a for a in range(3) if 0 <= z + a - 1 < depth]
        left = jnp.concatenate([w_ref[a * 3 + b] for a in taps for b in range(3)], axis=1)
        views = [
            windows([channels(refs, cells, (z + a - 1) * height + y) for y in range(height)])
            for a in taps
        ]
        for y in range(height // 2):
            right = jnp.concatenate([w for view in views for w in view[y]], axis=0)
            yield z, y, jnp.dot(left, right, preferred_element_type=f32)


def combine(total, k, filters, across):
    part = total[:, k * across : (k + 1) * across]
    lane = lax.broadcasted_iota(jnp.int32, (filters, across), 1)
    left = pltpu.roll(part[:filters], 1, 1)
    right = pltpu.roll(part[2 * filters :], across - 1, 1)
    v = part[filters : 2 * filters]
    v += jnp.where(lane > 0, left, 0.0)
    return v + jnp.where(lane < across - 1, right, 0.0)


def own_parity(w_ref, *refs, depth, height, blocks):
    refs, sum_ref = (*refs[1:blocks], refs[0]), refs[-1]
    for z, y, total in products(w_ref, refs, depth, height):
        sum_ref[z * (height // 2) + y] = total


def other_parity(w_ref, bias_ref, sum_ref, *refs, depth, height):
    refs, v_ref = refs[:-1], refs[-1]
    filters, across = bias_ref.shape
    for z, y, total in products(w_ref, refs, depth, height):
        total += sum_ref[z * (height // 2) + y]
        for j in range(2):
            v_ref[z * height + 2 * y + j] = combine(total, j, filters, across) + bias_ref[...]


def finish(flags_ref, w_mine_ref, w_theirs_ref, v_ref, *refs, depth, height, count):
    refs, out_ref = refs[:-1], refs[-1]
    filters, across = v_ref.shape[1:]
    extra = 1 if count == 2 else 2
    beside = []
    for which in range(extra):
        tap = 2 * which if extra == 2 else jnp.where(flags_ref[2] > 0, 0, 2)
        left = jnp.concatenate(
            [w[tap * 3 + b] for b in range(3) for w in (w_mine_ref, w_theirs_ref)], axis=1
        )
        rows = [channels(refs, extra * height, which * height + y) for y in range(height)]
        added = []
        for view in windows(rows):
            total = jnp.dot(left, jnp.concatenate(view, axis=0), preferred_element_type=f32)
            added += [combine(total, j, filters, across) for j in range(2)]
        beside.append(added)
    pooled = {}
    for z in range(depth):
        for y in range(height):
            v = v_ref[z * height + y]
            if z == 0:
                v += jnp.where(flags_ref[2] > 0, beside[0][y], 0.0)
            if z == depth - 1:
                v += jnp.where(flags_ref[3] > 0, beside[-1][y], 0.0)
            v = jnp.where(v > 0, v, slope * v)
            key = (z // 2, y // 2)
            pooled[key] = v if key not in pooled else jnp.maximum(pooled[key], v)
    stacked = jnp.concatenate(
        [pooled[z, y] for z in range(depth // 2) for y in range(height // 2)], axis=0
    )
    stacked = jnp.maximum(stacked, pltpu.roll(stacked, across - 1, 1)).astype(bf16)
    cells = (depth // 2) * (height // 2)
    size = cells * filters
    shift = cells.bit_length() - 1
    rows_pick = one_hot((size, size), lambda t: (t & (cells - 1)) * filters + (t >> shift))
    lane_from = lax.broadcasted_iota(jnp.int32, (across, across // 2), 0)
    lane_to = lax.broadcasted_iota(jnp.int32, (across, across // 2), 1)
    lanes_pick = jnp.where(lane_from == 2 * lane_to, 1.0, 0.0).astype(bf16)
    picked = jnp.dot(stacked, lanes_pick, preferred_element_type=f32).astype(bf16)
    out_ref[...] = jnp.dot(rows_pick, picked, preferred_element_type=f32).astype(bf16)


def shifted(x, relative, step, size, count):
    pairs = []
    for f in range(size):
        for s in range(count):
            t = 1 - s if step == "swap" else s + step
            if 0 <= t < count:
                pairs.append((f * count + s, (f ^ (2 * relative)) * count + t))
    return lax.ppermute(x, ("filt", "space"), pairs)


def on_device(volume, kernel, filter_bias):
    block, depth, height, across = volume.shape
    filters, cin = kernel.shape[0], kernel.shape[-1]
    size = lax.axis_size("filt")
    count = lax.axis_size("space")
    here = lax.axis_index("space")
    place = lax.axis_index("filt")
    flags = jnp.stack([place & 1, place >> 1, here, count - 1 - here]).astype(jnp.int32)
    far = size // 4
    pairs = height // 2
    cells = depth * height * block
    beside = height * block
    steps = ["swap"] if count == 2 else [1, -1]
    extra = len(steps)

    vmem = pl.BlockSpec(memory_space=pltpu.VMEM)
    smem = pl.BlockSpec(memory_space=pltpu.SMEM)
    hbm = pl.BlockSpec(memory_space=pltpu.HBM)
    anywhere = pl.BlockSpec(memory_space=pl.ANY)
    shape = jax.ShapeDtypeStruct

    def call(body, outs, ins, args, scratch=(), cost=12):
        return pl.pallas_call(
            body,
            out_shape=outs,
            in_specs=ins,
            out_specs=jax.tree.map(lambda _: vmem, outs),
            scratch_shapes=scratch,
            compiler_params=pltpu.CompilerParams(vmem_limit_bytes=16 << 20),
            cost_estimate=pl.CostEstimate(flops=1 << cost, bytes_accessed=1 << 8, transcendentals=0),
        )(*args)

    far_block = shifted(volume, far, 0, size, count)
    weights = kernel.transpose(1, 2, 3, 0, 4).reshape(-1, cin)
    given = [volume.reshape(cells, across), weights, filter_bias[None]]
    own_block, *edges, weights, bias = call(
        functools.partial(begin, block=block, depth=depth, count=count),
        [shape((cells, across), bf16)]
        + [shape((beside, across), bf16)] * extra
        + [shape(weights.shape, bf16), shape((1, filters), bf16)],
        [smem, hbm, hbm, hbm],
        [flags] + [pltpu.with_memory_space_constraint(x, pltpu.HBM) for x in given],
        [pltpu.SemaphoreType.DMA((3,))],
    )
    sends = list(zip(edges, steps))
    far_planes = [shifted(x, far, step, size, count) for x, step in sends]
    own_planes = [shifted(x, 0, step, size, count) for x, step in sends]
    pair = call(
        functools.partial(assemble, block=block),
        shape((2 * cells, across), bf16),
        [vmem, vmem],
        (own_block, far_block.reshape(cells, across)),
        cost=31,
    )
    ordered = shape((9, 3 * filters, cin // 2), bf16)
    w_mine, w_theirs, bias = call(
        functools.partial(prepare, block=block),
        (ordered, ordered, shape((filters, across), f32)),
        [smem, anywhere, vmem, vmem],
        (flags, pair, weights, bias),
        cost=31,
    )
    planes = call(
        join,
        shape((2 * extra * beside, across), bf16),
        [anywhere] + [vmem] * (2 * extra),
        [w_mine] + own_planes + far_planes,
        cost=31,
    )

    def near(x):
        parts = {r: shifted(x, r, 0, size, count) for r in [far - 1, *range(1, far - 1)]}
        return [x.reshape(-1, block, across)] + [
            parts[r].reshape(-1, block, across) for r in range(1, far)
        ]

    def swapped(x):
        return lax.ppermute(x, "filt", [(i, i ^ 1) for i in range(size)])

    mine = near(pair)
    theirs = [swapped(x) for x in mine]
    dims = dict(depth=depth, height=height)
    again = call(join, shape(planes.shape, bf16), [anywhere, vmem], (mine[-1], planes), cost=12)
    behind = [shifted(planes, r, 0, size, count) for r in range(2, far)]
    behind = [planes, shifted(again, 1, 0, size, count)] + behind
    partial = call(
        functools.partial(own_parity, blocks=far, **dims),
        shape((depth * pairs, 3 * filters, 2 * across), f32),
        [vmem] * (1 + far) + [anywhere] * (far - 2),
        [w_mine, mine[-1]] + mine[:-1] + behind[2:],
        cost=28,
    )
    planes = call(
        join,
        shape((far * planes.shape[0], across), bf16),
        [anywhere] + [vmem] * far,
        [partial] + behind,
    ).reshape(-1, block, across)
    v = call(
        functools.partial(other_parity, **dims),
        shape((depth * height, filters, across), f32),
        [vmem] * (3 + far),
        [w_theirs, bias, partial] + theirs,
    )
    pooled = call(
        functools.partial(finish, count=count, **dims),
        shape((filters * depth * height // 4, across // 2), bf16),
        [smem] + [vmem] * 5,
        (flags, w_mine, w_theirs, v, planes, swapped(planes)),
    )
    return pooled.reshape(filters, depth // 2, height // 2, across // 2)


def solution(mesh):
    in_specs = (P("filt", "space", None, None), P("filt", None, None, None, None), P("filt"))
    out_specs = P("filt", "space", None, None)
    return jax.shard_map(
        on_device, mesh=mesh, in_specs=in_specs, out_specs=out_specs, check_vma=False
    )
```

```python
import functools

import jax
import jax.numpy as jnp
from jax import lax
from jax.experimental import pallas as pl
from jax.experimental.pallas import tpu as pltpu
from jax.sharding import PartitionSpec as P

slope = 0.3
f32, bf16 = jnp.float32, jnp.bfloat16


def one_hot(shape, wanted):
    target = lax.broadcasted_iota(jnp.int32, (shape[0], 1), 0)
    source = lax.broadcasted_iota(jnp.int32, shape, 1)
    return jnp.where(source == wanted(target), 1.0, 0.0).astype(bf16)


def pick_rows(x, block, count, first):
    rows = x.shape[0]
    cells = rows // block
    shift = block.bit_length() - 1
    pick = one_hot(
        (count * block, rows), lambda t: (t & (block - 1)) * cells + (t >> shift) + first
    )
    return jnp.dot(pick, x, preferred_element_type=f32).astype(bf16)


def begin(vol_ref, bias_ref, own_ref, *refs, block, depth, count):
    plane_refs, (bias_out_ref, done) = refs[:-2], refs[-2:]
    copies = [
        pltpu.make_async_copy(source, target, done.at[k])
        for k, (source, target) in enumerate(
            [(vol_ref, own_ref), (bias_ref, bias_out_ref)]
        )
    ]
    for copy in copies:
        copy.start()
    height = own_ref.shape[0] // block // depth
    last = (depth - 1) * height
    copies[0].wait()
    if count == 2:
        firsts = [jnp.where(lax.axis_index("space") == 0, last, 0)]
    else:
        firsts = [last, 0]
    for ref, first in zip(plane_refs, firsts):
        ref[...] = pick_rows(own_ref[...], block, height, first)
    for copy in copies[1:]:
        copy.wait()


def prepare(
    _, w_ref, bias_ref, w_mine_ref, w_theirs_ref, bias_out_ref, kernel_ref, done, *, block
):
    fetch = pltpu.make_async_copy(w_ref, kernel_ref, done)
    fetch.start()
    cin = kernel_ref.shape[-1]
    half = cin // 2
    far = half // block // 2
    shift = block.bit_length() - 1
    place = lax.axis_index("filt")
    core, group = place & 1, place >> 1
    source = lax.broadcasted_iota(jnp.int32, (cin, cin), 0)
    target = lax.broadcasted_iota(jnp.int32, (1, cin), 1)
    part = jnp.where(target < half, core, 1 - core)
    slot = (target & (half - 1)) >> shift
    relative = (slot >> 1) | jnp.where((slot & 1) > 0, far, 0)
    wanted = ((((relative ^ group) << 1) | part) << shift) | (target & (block - 1))
    shuffle = jnp.where(source == wanted, 1.0, 0.0).astype(bf16)
    filters = bias_ref.shape[1]
    row = lax.broadcasted_iota(jnp.int32, (filters, filters), 0)
    column = lax.broadcasted_iota(jnp.int32, (filters, filters), 1)
    spread = jnp.where(row == column, bias_ref[...].astype(f32), 0.0)
    bias_out_ref[...] = jnp.broadcast_to(
        jnp.sum(spread, axis=1, keepdims=True), bias_out_ref.shape
    )
    fetch.wait()
    ordered = jnp.dot(kernel_ref[...], shuffle, preferred_element_type=f32).astype(bf16)
    w_mine_ref[...] = ordered[:, :half].reshape(w_mine_ref.shape)
    w_theirs_ref[...] = ordered[:, half:].reshape(w_theirs_ref.shape)


def assemble(own_ref, far_ref, pair_ref, *, block):
    size, across = own_ref.shape
    both = jnp.concatenate([own_ref[...], far_ref[...]], axis=1)
    moved = pick_rows(both, block, size // block, 0)
    pair_ref[:size] = moved[:, :across]
    pair_ref[size:] = moved[:, across:]


def join(*refs):
    in_refs, out_ref = refs[1:-1], refs[-1]
    at = 0
    for ref in in_refs:
        out_ref[at : at + ref.shape[0]] = ref[...]
        at += ref.shape[0]


def channels(refs, per_block, row):
    return jnp.concatenate(
        [ref[k * per_block + row] for ref in refs for k in range(ref.shape[0] // per_block)],
        axis=0,
    )


def windows(rows):
    zero = jnp.zeros_like(rows[0])
    rows = [zero] + rows + [zero]
    return [
        [jnp.concatenate([rows[y + b], rows[y + b + 1]], axis=1) for b in range(3)]
        for y in range(0, len(rows) - 2, 2)
    ]


def products(w_ref, refs, depth, height):
    cells = depth * height
    for z in range(depth):
        taps = [a for a in range(3) if 0 <= z + a - 1 < depth]
        left = jnp.concatenate([w_ref[a * 3 + b] for a in taps for b in range(3)], axis=1)
        views = [
            windows([channels(refs, cells, (z + a - 1) * height + y) for y in range(height)])
            for a in taps
        ]
        for y in range(height // 2):
            right = jnp.concatenate([w for view in views for w in view[y]], axis=0)
            yield z, y, jnp.dot(left, right, preferred_element_type=f32)


def combine(total, k, filters, across):
    part = total[:, k * across : (k + 1) * across]
    lane = lax.broadcasted_iota(jnp.int32, (filters, across), 1)
    left = pltpu.roll(part[:filters], 1, 1)
    right = pltpu.roll(part[2 * filters :], across - 1, 1)
    v = part[filters : 2 * filters]
    v += jnp.where(lane > 0, left, 0.0)
    return v + jnp.where(lane < across - 1, right, 0.0)


def own_parity(w_ref, *refs, depth, height, blocks):
    refs, sum_ref = (*refs[1:blocks], refs[0]), refs[-1]
    for z, y, total in products(w_ref, refs, depth, height):
        sum_ref[z * (height // 2) + y] = total


def other_parity(w_ref, bias_ref, sum_ref, *refs, depth, height):
    refs, v_ref = refs[:-1], refs[-1]
    filters, across = bias_ref.shape
    for z, y, total in products(w_ref, refs, depth, height):
        total += sum_ref[z * (height // 2) + y]
        for j in range(2):
            v_ref[z * height + 2 * y + j] = combine(total, j, filters, across) + bias_ref[...]


def finish(w_mine_ref, w_theirs_ref, v_ref, *refs, depth, height, count):
    refs, out_ref = refs[:-1], refs[-1]
    filters, across = v_ref.shape[1:]
    here = lax.axis_index("space")
    extra = 1 if count == 2 else 2
    beside = []
    for which in range(extra):
        tap = 2 * which if extra == 2 else jnp.where(here > 0, 0, 2)
        left = jnp.concatenate(
            [w[tap * 3 + b] for b in range(3) for w in (w_mine_ref, w_theirs_ref)], axis=1
        )
        rows = [channels(refs, extra * height, which * height + y) for y in range(height)]
        added = []
        for view in windows(rows):
            total = jnp.dot(left, jnp.concatenate(view, axis=0), preferred_element_type=f32)
            added += [combine(total, j, filters, across) for j in range(2)]
        beside.append(added)
    pooled = {}
    for z in range(depth):
        for y in range(height):
            v = v_ref[z * height + y]
            if z == 0:
                v += jnp.where(here > 0, beside[0][y], 0.0)
            if z == depth - 1:
                v += jnp.where(here < count - 1, beside[-1][y], 0.0)
            v = jnp.where(v > 0, v, slope * v)
            key = (z // 2, y // 2)
            pooled[key] = v if key not in pooled else jnp.maximum(pooled[key], v)
    stacked = jnp.concatenate(
        [pooled[z, y] for z in range(depth // 2) for y in range(height // 2)], axis=0
    )
    stacked = jnp.maximum(stacked, pltpu.roll(stacked, across - 1, 1)).astype(bf16)
    cells = (depth // 2) * (height // 2)
    size = cells * filters
    shift = cells.bit_length() - 1
    rows_pick = one_hot((size, size), lambda t: (t & (cells - 1)) * filters + (t >> shift))
    lane_from = lax.broadcasted_iota(jnp.int32, (across, across // 2), 0)
    lane_to = lax.broadcasted_iota(jnp.int32, (across, across // 2), 1)
    lanes_pick = jnp.where(lane_from == 2 * lane_to, 1.0, 0.0).astype(bf16)
    picked = jnp.dot(stacked, lanes_pick, preferred_element_type=f32).astype(bf16)
    out_ref[...] = jnp.dot(rows_pick, picked, preferred_element_type=f32).astype(bf16)


def shifted(x, relative, step, size, count):
    pairs = []
    for f in range(size):
        for s in range(count):
            t = 1 - s if step == "swap" else s + step
            if 0 <= t < count:
                pairs.append((f * count + s, (f ^ (2 * relative)) * count + t))
    return lax.ppermute(x, ("filt", "space"), pairs)


def on_device(volume, kernel, filter_bias):
    block, depth, height, across = volume.shape
    filters, cin = kernel.shape[0], kernel.shape[-1]
    size = lax.axis_size("filt")
    count = lax.axis_size("space")
    far = size // 4
    pairs = height // 2
    cells = depth * height * block
    beside = height * block
    steps = ["swap"] if count == 2 else [1, -1]
    extra = len(steps)

    vmem = pl.BlockSpec(memory_space=pltpu.VMEM)
    hbm = pl.BlockSpec(memory_space=pltpu.HBM)
    anywhere = pl.BlockSpec(memory_space=pl.ANY)
    shape = jax.ShapeDtypeStruct

    def call(body, outs, ins, args, scratch=(), cost=12):
        return pl.pallas_call(
            body,
            out_shape=outs,
            in_specs=ins,
            out_specs=jax.tree.map(lambda _: vmem, outs),
            scratch_shapes=scratch,
            compiler_params=pltpu.CompilerParams(vmem_limit_bytes=16 << 20),
            cost_estimate=pl.CostEstimate(flops=1 << cost, bytes_accessed=1 << 8, transcendentals=0),
        )(*args)

    def pinned(x):
        return pltpu.with_memory_space_constraint(x, pltpu.HBM)

    far_block = shifted(volume, far, 0, size, count)
    weights = kernel.transpose(1, 2, 3, 0, 4).reshape(-1, cin)
    own_block, *edges, bias = call(
        functools.partial(begin, block=block, depth=depth, count=count),
        [shape((cells, across), bf16)]
        + [shape((beside, across), bf16)] * extra
        + [shape((1, filters), bf16)],
        [hbm, hbm],
        (pinned(volume.reshape(cells, across)), pinned(filter_bias[None])),
        [pltpu.SemaphoreType.DMA((2,))],
    )
    sends = list(zip(edges, steps))
    far_planes = [shifted(x, far, step, size, count) for x, step in sends]
    own_planes = [shifted(x, 0, step, size, count) for x, step in sends]
    pair = call(
        functools.partial(assemble, block=block),
        shape((2 * cells, across), bf16),
        [vmem, vmem],
        (own_block, far_block.reshape(cells, across)),
        cost=31,
    )
    ordered = shape((9, 3 * filters, cin // 2), bf16)
    w_mine, w_theirs, bias = call(
        functools.partial(prepare, block=block),
        (ordered, ordered, shape((filters, across), f32)),
        [anywhere, hbm, vmem],
        (pair, pinned(weights), bias),
        [pltpu.VMEM(weights.shape, bf16), pltpu.SemaphoreType.DMA(())],
        cost=31,
    )
    planes = call(
        join,
        shape((2 * extra * beside, across), bf16),
        [anywhere] + [vmem] * (2 * extra),
        [w_mine] + own_planes + far_planes,
        cost=31,
    )

    def near(x):
        parts = {r: shifted(x, r, 0, size, count) for r in [far - 1, *range(1, far - 1)]}
        return [x.reshape(-1, block, across)] + [
            parts[r].reshape(-1, block, across) for r in range(1, far)
        ]

    def swapped(x):
        return lax.ppermute(x, "filt", [(i, i ^ 1) for i in range(size)])

    mine = near(pair)
    theirs = [swapped(x) for x in mine]
    dims = dict(depth=depth, height=height)
    again = call(join, shape(planes.shape, bf16), [anywhere, vmem], (mine[-1], planes), cost=12)
    behind = [shifted(planes, r, 0, size, count) for r in range(2, far)]
    behind = [planes, shifted(again, 1, 0, size, count)] + behind
    partial = call(
        functools.partial(own_parity, blocks=far, **dims),
        shape((depth * pairs, 3 * filters, 2 * across), f32),
        [vmem] * (1 + far),
        [w_mine, mine[-1]] + mine[:-1],
        cost=28,
    )
    planes = call(
        join,
        shape((far * planes.shape[0], across), bf16),
        [anywhere] + [vmem] * far,
        [partial] + behind,
    ).reshape(-1, block, across)
    v = call(
        functools.partial(other_parity, **dims),
        shape((depth * height, filters, across), f32),
        [vmem] * (3 + far),
        [w_theirs, bias, partial] + theirs,
    )
    pooled = call(
        functools.partial(finish, count=count, **dims),
        shape((filters * depth * height // 4, across // 2), bf16),
        [vmem] * 5,
        (w_mine, w_theirs, v, planes, swapped(planes)),
    )
    return pooled.reshape(filters, depth // 2, height // 2, across // 2)


def solution(mesh):
    in_specs = (P("filt", "space", None, None), P("filt", None, None, None, None), P("filt"))
    out_specs = P("filt", "space", None, None)
    return jax.shard_map(
        on_device, mesh=mesh, in_specs=in_specs, out_specs=out_specs, check_vma=False
    )
```

```python
import functools

import jax
import jax.numpy as jnp
from jax import lax
from jax.experimental import pallas as pl
from jax.experimental.pallas import tpu as pltpu
from jax.sharding import PartitionSpec as P

slope = 0.3
f32, bf16 = jnp.float32, jnp.bfloat16


def one_hot(shape, wanted):
    target = lax.broadcasted_iota(jnp.int32, (shape[0], 1), 0)
    source = lax.broadcasted_iota(jnp.int32, shape, 1)
    return jnp.where(source == wanted(target), 1.0, 0.0).astype(bf16)


def pick_rows(x, block, count, first):
    rows = x.shape[0]
    cells = rows // block
    shift = block.bit_length() - 1
    pick = one_hot(
        (count * block, rows), lambda t: (t & (block - 1)) * cells + (t >> shift) + first
    )
    return jnp.dot(pick, x, preferred_element_type=f32).astype(bf16)


def begin(vol_ref, bias_ref, own_ref, *refs, block, depth, count):
    plane_refs, (bias_out_ref, done) = refs[:-2], refs[-2:]
    copies = [
        pltpu.make_async_copy(source, target, done.at[k])
        for k, (source, target) in enumerate(
            [(vol_ref, own_ref), (bias_ref, bias_out_ref)]
        )
    ]
    for copy in copies:
        copy.start()
    height = own_ref.shape[0] // block // depth
    last = (depth - 1) * height
    copies[0].wait()
    if count == 2:
        firsts = [jnp.where(lax.axis_index("space") == 0, last, 0)]
    else:
        firsts = [last, 0]
    for ref, first in zip(plane_refs, firsts):
        ref[...] = pick_rows(own_ref[...], block, height, first)
    for copy in copies[1:]:
        copy.wait()


def prepare(
    _, w_ref, bias_ref, w_mine_ref, w_theirs_ref, bias_out_ref, kernel_ref, done, *, block
):
    fetch = pltpu.make_async_copy(w_ref, kernel_ref, done)
    fetch.start()
    cin = kernel_ref.shape[-1]
    half = cin // 2
    far = half // block // 2
    shift = block.bit_length() - 1
    place = lax.axis_index("filt")
    core, group = place & 1, place >> 1
    source = lax.broadcasted_iota(jnp.int32, (cin, cin), 0)
    target = lax.broadcasted_iota(jnp.int32, (1, cin), 1)
    part = jnp.where(target < half, core, 1 - core)
    slot = (target & (half - 1)) >> shift
    relative = (slot >> 1) | jnp.where((slot & 1) > 0, far, 0)
    wanted = ((((relative ^ group) << 1) | part) << shift) | (target & (block - 1))
    shuffle = jnp.where(source == wanted, 1.0, 0.0).astype(bf16)
    filters = bias_ref.shape[1]
    row = lax.broadcasted_iota(jnp.int32, (filters, filters), 0)
    column = lax.broadcasted_iota(jnp.int32, (filters, filters), 1)
    spread = jnp.where(row == column, bias_ref[...].astype(f32), 0.0)
    bias_out_ref[...] = jnp.broadcast_to(
        jnp.sum(spread, axis=1, keepdims=True), bias_out_ref.shape
    )
    fetch.wait()
    ordered = jnp.dot(kernel_ref[...], shuffle, preferred_element_type=f32).astype(bf16)
    w_mine_ref[...] = ordered[:, :half].reshape(w_mine_ref.shape)
    w_theirs_ref[...] = ordered[:, half:].reshape(w_theirs_ref.shape)


def assemble(own_ref, far_ref, pair_ref, *, block):
    size, across = own_ref.shape
    both = jnp.concatenate([own_ref[...], far_ref[...]], axis=1)
    moved = pick_rows(both, block, size // block, 0)
    pair_ref[:size] = moved[:, :across]
    pair_ref[size:] = moved[:, across:]


def join(*refs):
    in_refs, out_ref = refs[1:-1], refs[-1]
    at = 0
    for ref in in_refs:
        out_ref[at : at + ref.shape[0]] = ref[...]
        at += ref.shape[0]


def channels(refs, per_block, row):
    return jnp.concatenate(
        [ref[k * per_block + row] for ref in refs for k in range(ref.shape[0] // per_block)],
        axis=0,
    )


def windows(rows):
    zero = jnp.zeros_like(rows[0])
    rows = [zero] + rows + [zero]
    return [
        [jnp.concatenate([rows[y + b], rows[y + b + 1]], axis=1) for b in range(3)]
        for y in range(0, len(rows) - 2, 2)
    ]


def products(w_ref, refs, depth, height):
    cells = depth * height
    for z in range(depth):
        taps = [a for a in range(3) if 0 <= z + a - 1 < depth]
        left = jnp.concatenate([w_ref[a * 3 + b] for a in taps for b in range(3)], axis=1)
        views = [
            windows([channels(refs, cells, (z + a - 1) * height + y) for y in range(height)])
            for a in taps
        ]
        for y in range(height // 2):
            right = jnp.concatenate([w for view in views for w in view[y]], axis=0)
            yield z, y, jnp.dot(left, right, preferred_element_type=f32)


def combine(total, k, filters, across):
    part = total[:, k * across : (k + 1) * across]
    lane = lax.broadcasted_iota(jnp.int32, (filters, across), 1)
    left = pltpu.roll(part[:filters], 1, 1)
    right = pltpu.roll(part[2 * filters :], across - 1, 1)
    v = part[filters : 2 * filters]
    v += jnp.where(lane > 0, left, 0.0)
    return v + jnp.where(lane < across - 1, right, 0.0)


def own_parity(w_ref, *refs, depth, height, blocks):
    refs, sum_ref = (*refs[1:blocks], refs[0]), refs[-1]
    for z, y, total in products(w_ref, refs, depth, height):
        sum_ref[z * (height // 2) + y] = total


def other_parity(w_ref, bias_ref, sum_ref, *refs, depth, height):
    refs, v_ref = refs[:-1], refs[-1]
    filters, across = bias_ref.shape
    for z, y, total in products(w_ref, refs, depth, height):
        total += sum_ref[z * (height // 2) + y]
        for j in range(2):
            v_ref[z * height + 2 * y + j] = combine(total, j, filters, across) + bias_ref[...]


def finish(w_mine_ref, w_theirs_ref, v_ref, *refs, depth, height, count):
    refs, out_ref = refs[:-1], refs[-1]
    filters, across = v_ref.shape[1:]
    here = lax.axis_index("space")
    extra = 1 if count == 2 else 2
    beside = []
    for which in range(extra):
        tap = 2 * which if extra == 2 else jnp.where(here > 0, 0, 2)
        left = jnp.concatenate(
            [w[tap * 3 + b] for b in range(3) for w in (w_mine_ref, w_theirs_ref)], axis=1
        )
        rows = [channels(refs, extra * height, which * height + y) for y in range(height)]
        added = []
        for view in windows(rows):
            total = jnp.dot(left, jnp.concatenate(view, axis=0), preferred_element_type=f32)
            added += [combine(total, j, filters, across) for j in range(2)]
        beside.append(added)
    pooled = {}
    for z in range(depth):
        for y in range(height):
            v = v_ref[z * height + y]
            if z == 0:
                v += jnp.where(here > 0, beside[0][y], 0.0)
            if z == depth - 1:
                v += jnp.where(here < count - 1, beside[-1][y], 0.0)
            v = jnp.where(v > 0, v, slope * v)
            key = (z // 2, y // 2)
            pooled[key] = v if key not in pooled else jnp.maximum(pooled[key], v)
    stacked = jnp.concatenate(
        [pooled[z, y] for z in range(depth // 2) for y in range(height // 2)], axis=0
    )
    stacked = jnp.maximum(stacked, pltpu.roll(stacked, across - 1, 1)).astype(bf16)
    cells = (depth // 2) * (height // 2)
    size = cells * filters
    shift = cells.bit_length() - 1
    rows_pick = one_hot((size, size), lambda t: (t & (cells - 1)) * filters + (t >> shift))
    lane_from = lax.broadcasted_iota(jnp.int32, (across, across // 2), 0)
    lane_to = lax.broadcasted_iota(jnp.int32, (across, across // 2), 1)
    lanes_pick = jnp.where(lane_from == 2 * lane_to, 1.0, 0.0).astype(bf16)
    picked = jnp.dot(stacked, lanes_pick, preferred_element_type=f32).astype(bf16)
    out_ref[...] = jnp.dot(rows_pick, picked, preferred_element_type=f32).astype(bf16)


def shifted(x, relative, step, size, count):
    pairs = []
    for f in range(size):
        for s in range(count):
            t = 1 - s if step == "swap" else s + step
            if 0 <= t < count:
                pairs.append((f * count + s, (f ^ (2 * relative)) * count + t))
    return lax.ppermute(x, ("filt", "space"), pairs)


def on_device(volume, kernel, filter_bias):
    block, depth, height, across = volume.shape
    filters, cin = kernel.shape[0], kernel.shape[-1]
    size = lax.axis_size("filt")
    count = lax.axis_size("space")
    far = size // 4
    pairs = height // 2
    cells = depth * height * block
    beside = height * block
    steps = ["swap"] if count == 2 else [1, -1]
    extra = len(steps)

    vmem = pl.BlockSpec(memory_space=pltpu.VMEM)
    hbm = pl.BlockSpec(memory_space=pltpu.HBM)
    anywhere = pl.BlockSpec(memory_space=pl.ANY)
    shape = jax.ShapeDtypeStruct

    def call(body, outs, ins, args, scratch=(), cost=12):
        return pl.pallas_call(
            body,
            out_shape=outs,
            in_specs=ins,
            out_specs=jax.tree.map(lambda _: vmem, outs),
            scratch_shapes=scratch,
            compiler_params=pltpu.CompilerParams(vmem_limit_bytes=16 << 20),
            cost_estimate=pl.CostEstimate(flops=1 << cost, bytes_accessed=1 << 8, transcendentals=0),
        )(*args)

    def pinned(x):
        return pltpu.with_memory_space_constraint(x, pltpu.HBM)

    far_block = shifted(volume, far, 0, size, count)
    weights = kernel.transpose(1, 2, 3, 0, 4).reshape(-1, cin)
    own_block, *edges, bias = call(
        functools.partial(begin, block=block, depth=depth, count=count),
        [shape((cells, across), bf16)]
        + [shape((beside, across), bf16)] * extra
        + [shape((1, filters), bf16)],
        [hbm, hbm],
        (pinned(volume.reshape(cells, across)), pinned(filter_bias[None])),
        [pltpu.SemaphoreType.DMA((2,))],
    )
    sends = list(zip(edges, steps))
    far_planes = [shifted(x, far, step, size, count) for x, step in sends]
    own_planes = [shifted(x, 0, step, size, count) for x, step in sends]
    pair = call(
        functools.partial(assemble, block=block),
        shape((2 * cells, across), bf16),
        [vmem, vmem],
        (own_block, far_block.reshape(cells, across)),
        cost=31,
    )
    planes = call(
        join,
        shape((2 * extra * beside, across), bf16),
        [anywhere] + [vmem] * (2 * extra),
        [pair] + own_planes + far_planes,
        cost=31,
    )

    ordered = shape((9, 3 * filters, cin // 2), bf16)
    w_mine, w_theirs, bias = call(
        functools.partial(prepare, block=block),
        (ordered, ordered, shape((filters, across), f32)),
        [anywhere, hbm, vmem],
        (planes, pinned(weights), bias),
        [pltpu.VMEM(weights.shape, bf16), pltpu.SemaphoreType.DMA(())],
        cost=31,
    )

    def near(x):
        parts = {r: shifted(x, r, 0, size, count) for r in [far - 1, *range(1, far - 1)]}
        return [x.reshape(-1, block, across)] + [
            parts[r].reshape(-1, block, across) for r in range(1, far)
        ]

    def swapped(x):
        return lax.ppermute(x, "filt", [(i, i ^ 1) for i in range(size)])

    mine = near(pair)
    first = call(join, shape(pair.shape, bf16), [anywhere, vmem], (w_mine, pair))
    theirs = [swapped(x) for x in [first.reshape(-1, block, across)] + mine[1:]]
    dims = dict(depth=depth, height=height)
    again = call(join, shape(planes.shape, bf16), [anywhere, vmem], (mine[-1], planes), cost=12)
    behind = [shifted(planes, r, 0, size, count) for r in range(2, far)]
    behind = [planes, shifted(again, 1, 0, size, count)] + behind
    partial = call(
        functools.partial(own_parity, blocks=far, **dims),
        shape((depth * pairs, 3 * filters, 2 * across), f32),
        [vmem] * (1 + far),
        [w_mine, mine[-1]] + mine[:-1],
        cost=28,
    )
    planes = call(
        join,
        shape((far * planes.shape[0], across), bf16),
        [anywhere] + [vmem] * far,
        [partial] + behind,
    ).reshape(-1, block, across)
    v = call(
        functools.partial(other_parity, **dims),
        shape((depth * height, filters, across), f32),
        [vmem] * (3 + far),
        [w_theirs, bias, partial] + theirs,
    )
    pooled = call(
        functools.partial(finish, count=count, **dims),
        shape((filters * depth * height // 4, across // 2), bf16),
        [vmem] * 5,
        (w_mine, w_theirs, v, planes, swapped(planes)),
    )
    return pooled.reshape(filters, depth // 2, height // 2, across // 2)


def solution(mesh):
    in_specs = (P("filt", "space", None, None), P("filt", None, None, None, None), P("filt"))
    out_specs = P("filt", "space", None, None)
    return jax.shard_map(
        on_device, mesh=mesh, in_specs=in_specs, out_specs=out_specs, check_vma=False
    )
```

```python
import functools

import jax
import jax.numpy as jnp
from jax import lax
from jax.experimental import pallas as pl
from jax.experimental.pallas import tpu as pltpu
from jax.sharding import PartitionSpec as P

slope = 0.3
f32, bf16 = jnp.float32, jnp.bfloat16


def one_hot(shape, wanted):
    target = lax.broadcasted_iota(jnp.int32, (shape[0], 1), 0)
    source = lax.broadcasted_iota(jnp.int32, shape, 1)
    return jnp.where(source == wanted(target), 1.0, 0.0).astype(bf16)


def pick_rows(x, block, count, first):
    rows = x.shape[0]
    cells = rows // block
    shift = block.bit_length() - 1
    pick = one_hot(
        (count * block, rows), lambda t: (t & (block - 1)) * cells + (t >> shift) + first
    )
    return jnp.dot(pick, x, preferred_element_type=f32).astype(bf16)


def begin(vol_ref, bias_ref, own_ref, *refs, block, depth, count):
    plane_refs, (bias_out_ref, done) = refs[:-2], refs[-2:]
    copies = [
        pltpu.make_async_copy(source, target, done.at[k])
        for k, (source, target) in enumerate(
            [(vol_ref, own_ref), (bias_ref, bias_out_ref)]
        )
    ]
    for copy in copies:
        copy.start()
    height = own_ref.shape[0] // block // depth
    last = (depth - 1) * height
    copies[0].wait()
    if count == 2:
        firsts = [jnp.where(lax.axis_index("space") == 0, last, 0)]
    else:
        firsts = [last, 0]
    for ref, first in zip(plane_refs, firsts):
        ref[...] = pick_rows(own_ref[...], block, height, first)
    for copy in copies[1:]:
        copy.wait()


def prepare(
    w_ref, bias_ref, w_mine_ref, w_theirs_ref, bias_out_ref, kernel_ref, done, *, block
):
    rows = w_ref.shape[0] // 9
    fetches = [
        pltpu.make_async_copy(
            w_ref.at[pl.ds(k * rows, rows)], kernel_ref.at[pl.ds(k * rows, rows)], done.at[k]
        )
        for k in range(9)
    ]
    for fetch in fetches:
        fetch.start()
    cin = kernel_ref.shape[-1]
    half = cin // 2
    far = half // block // 2
    shift = block.bit_length() - 1
    place = lax.axis_index("filt")
    core, group = place & 1, place >> 1
    source = lax.broadcasted_iota(jnp.int32, (cin, cin), 0)
    target = lax.broadcasted_iota(jnp.int32, (1, cin), 1)
    part = jnp.where(target < half, core, 1 - core)
    slot = (target & (half - 1)) >> shift
    relative = (slot >> 1) | jnp.where((slot & 1) > 0, far, 0)
    wanted = ((((relative ^ group) << 1) | part) << shift) | (target & (block - 1))
    shuffle = jnp.where(source == wanted, 1.0, 0.0).astype(bf16)
    filters = bias_ref.shape[1]
    row = lax.broadcasted_iota(jnp.int32, (filters, filters), 0)
    column = lax.broadcasted_iota(jnp.int32, (filters, filters), 1)
    spread = jnp.where(row == column, bias_ref[...].astype(f32), 0.0)
    bias_out_ref[...] = jnp.broadcast_to(
        jnp.sum(spread, axis=1, keepdims=True), bias_out_ref.shape
    )
    for fetch in fetches:
        fetch.wait()
    ordered = jnp.dot(kernel_ref[...], shuffle, preferred_element_type=f32).astype(bf16)
    w_mine_ref[...] = ordered[:, :half].reshape(w_mine_ref.shape)
    w_theirs_ref[...] = ordered[:, half:].reshape(w_theirs_ref.shape)


def assemble(_, own_ref, far_ref, pair_ref, *, block):
    size, across = own_ref.shape
    both = jnp.concatenate([own_ref[...], far_ref[...]], axis=1)
    moved = pick_rows(both, block, size // block, 0)
    pair_ref[:size] = moved[:, :across]
    pair_ref[size:] = moved[:, across:]


def join(*refs):
    in_refs, out_ref = refs[1:-1], refs[-1]
    at = 0
    for ref in in_refs:
        out_ref[at : at + ref.shape[0]] = ref[...]
        at += ref.shape[0]


def channels(refs, per_block, row):
    return jnp.concatenate(
        [ref[k * per_block + row] for ref in refs for k in range(ref.shape[0] // per_block)],
        axis=0,
    )


def windows(rows):
    zero = jnp.zeros_like(rows[0])
    rows = [zero] + rows + [zero]
    return [
        [jnp.concatenate([rows[y + b], rows[y + b + 1]], axis=1) for b in range(3)]
        for y in range(0, len(rows) - 2, 2)
    ]


def products(w_ref, refs, depth, height):
    cells = depth * height
    for z in range(depth):
        taps = [a for a in range(3) if 0 <= z + a - 1 < depth]
        left = jnp.concatenate([w_ref[a * 3 + b] for a in taps for b in range(3)], axis=1)
        views = [
            windows([channels(refs, cells, (z + a - 1) * height + y) for y in range(height)])
            for a in taps
        ]
        for y in range(height // 2):
            right = jnp.concatenate([w for view in views for w in view[y]], axis=0)
            yield z, y, jnp.dot(left, right, preferred_element_type=f32)


def combine(total, k, filters, across):
    part = total[:, k * across : (k + 1) * across]
    lane = lax.broadcasted_iota(jnp.int32, (filters, across), 1)
    left = pltpu.roll(part[:filters], 1, 1)
    right = pltpu.roll(part[2 * filters :], across - 1, 1)
    v = part[filters : 2 * filters]
    v += jnp.where(lane > 0, left, 0.0)
    return v + jnp.where(lane < across - 1, right, 0.0)


def own_parity(w_ref, *refs, depth, height, blocks):
    refs, sum_ref = (*refs[1:blocks], refs[0]), refs[-1]
    for z, y, total in products(w_ref, refs, depth, height):
        sum_ref[z * (height // 2) + y] = total


def other_parity(w_ref, bias_ref, sum_ref, *refs, depth, height):
    refs, v_ref = refs[:-1], refs[-1]
    filters, across = bias_ref.shape
    for z, y, total in products(w_ref, refs, depth, height):
        total += sum_ref[z * (height // 2) + y]
        for j in range(2):
            v_ref[z * height + 2 * y + j] = combine(total, j, filters, across) + bias_ref[...]


def finish(w_mine_ref, w_theirs_ref, v_ref, *refs, depth, height, count):
    refs, out_ref = refs[:-1], refs[-1]
    filters, across = v_ref.shape[1:]
    here = lax.axis_index("space")
    extra = 1 if count == 2 else 2
    beside = []
    for which in range(extra):
        tap = 2 * which if extra == 2 else jnp.where(here > 0, 0, 2)
        left = jnp.concatenate(
            [w[tap * 3 + b] for b in range(3) for w in (w_mine_ref, w_theirs_ref)], axis=1
        )
        rows = [channels(refs, extra * height, which * height + y) for y in range(height)]
        added = []
        for view in windows(rows):
            total = jnp.dot(left, jnp.concatenate(view, axis=0), preferred_element_type=f32)
            added += [combine(total, j, filters, across) for j in range(2)]
        beside.append(added)
    pooled = {}
    for z in range(depth):
        for y in range(height):
            v = v_ref[z * height + y]
            if z == 0:
                v += jnp.where(here > 0, beside[0][y], 0.0)
            if z == depth - 1:
                v += jnp.where(here < count - 1, beside[-1][y], 0.0)
            v = jnp.where(v > 0, v, slope * v)
            key = (z // 2, y // 2)
            pooled[key] = v if key not in pooled else jnp.maximum(pooled[key], v)
    stacked = jnp.concatenate(
        [pooled[z, y] for z in range(depth // 2) for y in range(height // 2)], axis=0
    )
    stacked = jnp.maximum(stacked, pltpu.roll(stacked, across - 1, 1)).astype(bf16)
    cells = (depth // 2) * (height // 2)
    size = cells * filters
    shift = cells.bit_length() - 1
    rows_pick = one_hot((size, size), lambda t: (t & (cells - 1)) * filters + (t >> shift))
    lane_from = lax.broadcasted_iota(jnp.int32, (across, across // 2), 0)
    lane_to = lax.broadcasted_iota(jnp.int32, (across, across // 2), 1)
    lanes_pick = jnp.where(lane_from == 2 * lane_to, 1.0, 0.0).astype(bf16)
    picked = jnp.dot(stacked, lanes_pick, preferred_element_type=f32).astype(bf16)
    out_ref[...] = jnp.dot(rows_pick, picked, preferred_element_type=f32).astype(bf16)


def shifted(x, relative, step, size, count):
    pairs = []
    for f in range(size):
        for s in range(count):
            t = 1 - s if step == "swap" else s + step
            if 0 <= t < count:
                pairs.append((f * count + s, (f ^ (2 * relative)) * count + t))
    return lax.ppermute(x, ("filt", "space"), pairs)


def on_device(volume, kernel, filter_bias):
    block, depth, height, across = volume.shape
    filters, cin = kernel.shape[0], kernel.shape[-1]
    size = lax.axis_size("filt")
    count = lax.axis_size("space")
    far = size // 4
    pairs = height // 2
    cells = depth * height * block
    beside = height * block
    steps = ["swap"] if count == 2 else [1, -1]
    extra = len(steps)

    vmem = pl.BlockSpec(memory_space=pltpu.VMEM)
    hbm = pl.BlockSpec(memory_space=pltpu.HBM)
    anywhere = pl.BlockSpec(memory_space=pl.ANY)
    shape = jax.ShapeDtypeStruct

    def call(body, outs, ins, args, scratch=(), cost=12):
        return pl.pallas_call(
            body,
            out_shape=outs,
            in_specs=ins,
            out_specs=jax.tree.map(lambda _: vmem, outs),
            scratch_shapes=scratch,
            compiler_params=pltpu.CompilerParams(vmem_limit_bytes=16 << 20),
            cost_estimate=pl.CostEstimate(flops=1 << cost, bytes_accessed=1 << 8, transcendentals=0),
        )(*args)

    def pinned(x):
        return pltpu.with_memory_space_constraint(x, pltpu.HBM)

    far_block = shifted(volume, far, 0, size, count)
    weights = kernel.transpose(1, 2, 3, 0, 4).reshape(-1, cin)
    own_block, *edges, bias = call(
        functools.partial(begin, block=block, depth=depth, count=count),
        [shape((cells, across), bf16)]
        + [shape((beside, across), bf16)] * extra
        + [shape((1, filters), bf16)],
        [hbm, hbm],
        (pinned(volume.reshape(cells, across)), pinned(filter_bias[None])),
        [pltpu.SemaphoreType.DMA((2,))],
    )
    sends = list(zip(edges, steps))
    far_planes = [shifted(x, far, step, size, count) for x, step in sends]
    own_planes = [shifted(x, 0, step, size, count) for x, step in sends]
    ordered = shape((9, 3 * filters, cin // 2), bf16)
    w_mine, w_theirs, bias = call(
        functools.partial(prepare, block=block),
        (ordered, ordered, shape((filters, across), f32)),
        [hbm, vmem],
        (pinned(weights), bias),
        [pltpu.VMEM(weights.shape, bf16), pltpu.SemaphoreType.DMA((9,))],
        cost=31,
    )

    pair = call(
        functools.partial(assemble, block=block),
        shape((2 * cells, across), bf16),
        [anywhere, vmem, vmem],
        (w_mine, own_block, far_block.reshape(cells, across)),
        cost=31,
    )
    planes = call(
        join,
        shape((2 * extra * beside, across), bf16),
        [anywhere] + [vmem] * (2 * extra),
        [pair] + own_planes + far_planes,
        cost=31,
    )

    def near(x):
        parts = {r: shifted(x, r, 0, size, count) for r in [far - 1, *range(1, far - 1)]}
        return [x.reshape(-1, block, across)] + [
            parts[r].reshape(-1, block, across) for r in range(1, far)
        ]

    def swapped(x):
        return lax.ppermute(x, "filt", [(i, i ^ 1) for i in range(size)])

    mine = near(pair)
    theirs = [swapped(x) for x in mine]
    dims = dict(depth=depth, height=height)
    again = call(join, shape(planes.shape, bf16), [anywhere, vmem], (mine[-1], planes), cost=12)
    behind = [shifted(planes, r, 0, size, count) for r in range(2, far)]
    behind = [planes, shifted(again, 1, 0, size, count)] + behind
    partial = call(
        functools.partial(own_parity, blocks=far, **dims),
        shape((depth * pairs, 3 * filters, 2 * across), f32),
        [vmem] * (1 + far),
        [w_mine, mine[-1]] + mine[:-1],
        cost=28,
    )
    planes = call(
        join,
        shape((far * planes.shape[0], across), bf16),
        [anywhere] + [vmem] * far,
        [partial] + behind,
    ).reshape(-1, block, across)
    v = call(
        functools.partial(other_parity, **dims),
        shape((depth * height, filters, across), f32),
        [vmem] * (3 + far),
        [w_theirs, bias, partial] + theirs,
    )
    pooled = call(
        functools.partial(finish, count=count, **dims),
        shape((filters * depth * height // 4, across // 2), bf16),
        [vmem] * 5,
        (w_mine, w_theirs, v, planes, swapped(planes)),
    )
    return pooled.reshape(filters, depth // 2, height // 2, across // 2)


def solution(mesh):
    in_specs = (P("filt", "space", None, None), P("filt", None, None, None, None), P("filt"))
    out_specs = P("filt", "space", None, None)
    return jax.shard_map(
        on_device, mesh=mesh, in_specs=in_specs, out_specs=out_specs, check_vma=False
    )
```

```python
import functools

import jax
import jax.numpy as jnp
from jax import lax
from jax.experimental import pallas as pl
from jax.experimental.pallas import tpu as pltpu
from jax.sharding import PartitionSpec as P

slope = 0.3
f32, bf16 = jnp.float32, jnp.bfloat16


def one_hot(shape, wanted):
    target = lax.broadcasted_iota(jnp.int32, (shape[0], 1), 0)
    source = lax.broadcasted_iota(jnp.int32, shape, 1)
    return jnp.where(source == wanted(target), 1.0, 0.0).astype(bf16)


def pick_rows(x, block, count, first):
    rows = x.shape[0]
    cells = rows // block
    shift = block.bit_length() - 1
    pick = one_hot(
        (count * block, rows), lambda t: (t & (block - 1)) * cells + (t >> shift) + first
    )
    return jnp.dot(pick, x, preferred_element_type=f32).astype(bf16)


def begin(vol_ref, bias_ref, own_ref, *refs, block, depth, count):
    plane_refs, (bias_out_ref, done) = refs[:-2], refs[-2:]
    copies = [
        pltpu.make_async_copy(source, target, done.at[k])
        for k, (source, target) in enumerate(
            [(vol_ref, own_ref), (bias_ref, bias_out_ref)]
        )
    ]
    for copy in copies:
        copy.start()
    height = own_ref.shape[0] // block // depth
    last = (depth - 1) * height
    copies[0].wait()
    if count == 2:
        firsts = [jnp.where(lax.axis_index("space") == 0, last, 0)]
    else:
        firsts = [last, 0]
    for ref, first in zip(plane_refs, firsts):
        ref[...] = pick_rows(own_ref[...], block, height, first)
    for copy in copies[1:]:
        copy.wait()


def prepare(
    w_ref, bias_ref, w_mine_ref, w_theirs_ref, bias_out_ref, kernel_ref, done, *, block
):
    rows = w_ref.shape[0] // 9
    fetches = [
        pltpu.make_async_copy(
            w_ref.at[pl.ds(k * rows, rows)], kernel_ref.at[pl.ds(k * rows, rows)], done.at[k]
        )
        for k in range(9)
    ]
    for fetch in fetches:
        fetch.start()
    cin = kernel_ref.shape[-1]
    half = cin // 2
    far = half // block // 2
    shift = block.bit_length() - 1
    place = lax.axis_index("filt")
    core, group = place & 1, place >> 1
    source = lax.broadcasted_iota(jnp.int32, (cin, cin), 0)
    target = lax.broadcasted_iota(jnp.int32, (1, cin), 1)
    part = jnp.where(target < half, core, 1 - core)
    slot = (target & (half - 1)) >> shift
    relative = (slot >> 1) | jnp.where((slot & 1) > 0, far, 0)
    wanted = ((((relative ^ group) << 1) | part) << shift) | (target & (block - 1))
    shuffle = jnp.where(source == wanted, 1.0, 0.0).astype(bf16)
    filters = bias_ref.shape[1]
    row = lax.broadcasted_iota(jnp.int32, (filters, filters), 0)
    column = lax.broadcasted_iota(jnp.int32, (filters, filters), 1)
    spread = jnp.where(row == column, bias_ref[...].astype(f32), 0.0)
    bias_out_ref[...] = jnp.broadcast_to(
        jnp.sum(spread, axis=1, keepdims=True), bias_out_ref.shape
    )
    for fetch in fetches:
        fetch.wait()
    ordered = jnp.dot(kernel_ref[...], shuffle, preferred_element_type=f32).astype(bf16)
    w_mine_ref[...] = ordered[:, :half].reshape(w_mine_ref.shape)
    w_theirs_ref[...] = ordered[:, half:].reshape(w_theirs_ref.shape)


def assemble(_, own_ref, far_ref, pair_ref, *, block):
    size, across = own_ref.shape
    both = jnp.concatenate([own_ref[...], far_ref[...]], axis=1)
    moved = pick_rows(both, block, size // block, 0)
    pair_ref[:size] = moved[:, :across]
    pair_ref[size:] = moved[:, across:]


def join(*refs):
    in_refs, out_ref = refs[1:-1], refs[-1]
    at = 0
    for ref in in_refs:
        out_ref[at : at + ref.shape[0]] = ref[...]
        at += ref.shape[0]


def channels(refs, per_block, row):
    return jnp.concatenate(
        [ref[k * per_block + row] for ref in refs for k in range(ref.shape[0] // per_block)],
        axis=0,
    )


def windows(rows):
    zero = jnp.zeros_like(rows[0])
    rows = [zero] + rows + [zero]
    return [
        [jnp.concatenate([rows[y + b], rows[y + b + 1]], axis=1) for b in range(3)]
        for y in range(0, len(rows) - 2, 2)
    ]


def products(w_ref, refs, depth, height):
    cells = depth * height
    for z in range(depth):
        taps = [a for a in range(3) if 0 <= z + a - 1 < depth]
        left = jnp.concatenate([w_ref[a * 3 + b] for a in taps for b in range(3)], axis=1)
        views = [
            windows([channels(refs, cells, (z + a - 1) * height + y) for y in range(height)])
            for a in taps
        ]
        for y in range(height // 2):
            right = jnp.concatenate([w for view in views for w in view[y]], axis=0)
            yield z, y, jnp.dot(left, right, preferred_element_type=f32)


def combine(total, k, filters, across):
    part = total[:, k * across : (k + 1) * across]
    lane = lax.broadcasted_iota(jnp.int32, (filters, across), 1)
    left = pltpu.roll(part[:filters], 1, 1)
    right = pltpu.roll(part[2 * filters :], across - 1, 1)
    v = part[filters : 2 * filters]
    v += jnp.where(lane > 0, left, 0.0)
    return v + jnp.where(lane < across - 1, right, 0.0)


def own_parity(w_ref, *refs, depth, height, blocks):
    refs, sum_ref = (*refs[1:blocks], refs[0]), refs[-1]
    for z, y, total in products(w_ref, refs, depth, height):
        sum_ref[z * (height // 2) + y] = total


def other_parity(w_ref, bias_ref, sum_ref, *refs, depth, height):
    refs, v_ref = refs[:-1], refs[-1]
    filters, across = bias_ref.shape
    for z, y, total in products(w_ref, refs, depth, height):
        total += sum_ref[z * (height // 2) + y]
        for j in range(2):
            v_ref[z * height + 2 * y + j] = combine(total, j, filters, across) + bias_ref[...]


def finish(w_mine_ref, w_theirs_ref, v_ref, *refs, depth, height, count):
    refs, out_ref = refs[:-1], refs[-1]
    filters, across = v_ref.shape[1:]
    here = lax.axis_index("space")
    extra = 1 if count == 2 else 2
    beside = []
    for which in range(extra):
        tap = 2 * which if extra == 2 else jnp.where(here > 0, 0, 2)
        left = jnp.concatenate(
            [w[tap * 3 + b] for b in range(3) for w in (w_mine_ref, w_theirs_ref)], axis=1
        )
        rows = [channels(refs, extra * height, which * height + y) for y in range(height)]
        added = []
        for view in windows(rows):
            total = jnp.dot(left, jnp.concatenate(view, axis=0), preferred_element_type=f32)
            added += [combine(total, j, filters, across) for j in range(2)]
        beside.append(added)
    pooled = {}
    for z in range(depth):
        for y in range(height):
            v = v_ref[z * height + y]
            if z == 0:
                v += jnp.where(here > 0, beside[0][y], 0.0)
            if z == depth - 1:
                v += jnp.where(here < count - 1, beside[-1][y], 0.0)
            v = jnp.where(v > 0, v, slope * v)
            key = (z // 2, y // 2)
            pooled[key] = v if key not in pooled else jnp.maximum(pooled[key], v)
    stacked = jnp.concatenate(
        [pooled[z, y] for z in range(depth // 2) for y in range(height // 2)], axis=0
    )
    stacked = jnp.maximum(stacked, pltpu.roll(stacked, across - 1, 1)).astype(bf16)
    cells = (depth // 2) * (height // 2)
    size = cells * filters
    shift = cells.bit_length() - 1
    rows_pick = one_hot((size, size), lambda t: (t & (cells - 1)) * filters + (t >> shift))
    lane_from = lax.broadcasted_iota(jnp.int32, (across, across // 2), 0)
    lane_to = lax.broadcasted_iota(jnp.int32, (across, across // 2), 1)
    lanes_pick = jnp.where(lane_from == 2 * lane_to, 1.0, 0.0).astype(bf16)
    picked = jnp.dot(stacked, lanes_pick, preferred_element_type=f32).astype(bf16)
    out_ref[...] = jnp.dot(rows_pick, picked, preferred_element_type=f32).astype(bf16)


def shifted(x, relative, step, size, count):
    pairs = []
    for f in range(size):
        for s in range(count):
            t = 1 - s if step == "swap" else s + step
            if 0 <= t < count:
                pairs.append((f * count + s, (f ^ (2 * relative)) * count + t))
    return lax.ppermute(x, ("filt", "space"), pairs)


def on_device(volume, kernel, filter_bias):
    block, depth, height, across = volume.shape
    filters, cin = kernel.shape[0], kernel.shape[-1]
    size = lax.axis_size("filt")
    count = lax.axis_size("space")
    far = size // 4
    pairs = height // 2
    cells = depth * height * block
    beside = height * block
    steps = ["swap"] if count == 2 else [1, -1]
    extra = len(steps)

    vmem = pl.BlockSpec(memory_space=pltpu.VMEM)
    hbm = pl.BlockSpec(memory_space=pltpu.HBM)
    anywhere = pl.BlockSpec(memory_space=pl.ANY)
    shape = jax.ShapeDtypeStruct

    def call(body, outs, ins, args, scratch=(), cost=12):
        return pl.pallas_call(
            body,
            out_shape=outs,
            in_specs=ins,
            out_specs=jax.tree.map(lambda _: vmem, outs),
            scratch_shapes=scratch,
            compiler_params=pltpu.CompilerParams(vmem_limit_bytes=16 << 20),
            cost_estimate=pl.CostEstimate(flops=1 << cost, bytes_accessed=1 << 8, transcendentals=0),
        )(*args)

    def pinned(x):
        return pltpu.with_memory_space_constraint(x, pltpu.HBM)

    far_block = shifted(volume, far, 0, size, count)
    weights = kernel.transpose(1, 2, 3, 0, 4).reshape(-1, cin)
    own_block, *edges, bias = call(
        functools.partial(begin, block=block, depth=depth, count=count),
        [shape((cells, across), bf16)]
        + [shape((beside, across), bf16)] * extra
        + [shape((1, filters), bf16)],
        [hbm, hbm],
        (pinned(volume.reshape(cells, across)), pinned(filter_bias[None])),
        [pltpu.SemaphoreType.DMA((2,))],
    )
    sends = list(zip(edges, steps))
    far_planes = [shifted(x, far, step, size, count) for x, step in sends]
    own_planes = [shifted(x, 0, step, size, count) for x, step in sends]
    ordered = shape((9, 3 * filters, cin // 2), bf16)
    w_mine, w_theirs, bias = call(
        functools.partial(prepare, block=block),
        (ordered, ordered, shape((filters, across), f32)),
        [hbm, vmem],
        (pinned(weights), bias),
        [pltpu.VMEM(weights.shape, bf16), pltpu.SemaphoreType.DMA((9,))],
        cost=31,
    )

    pair = call(
        functools.partial(assemble, block=block),
        shape((2 * cells, across), bf16),
        [anywhere, vmem, vmem],
        (w_mine, own_block, far_block.reshape(cells, across)),
        cost=31,
    )
    planes = call(
        join,
        shape((2 * extra * beside, across), bf16),
        [anywhere] + [vmem] * (2 * extra),
        [pair] + own_planes + far_planes,
        cost=31,
    )

    def near(x):
        parts = {r: shifted(x, r, 0, size, count) for r in [far - 1, *range(1, far - 1)]}
        return [x.reshape(-1, block, across)] + [
            parts[r].reshape(-1, block, across) for r in range(1, far)
        ]

    def swapped(x):
        return lax.ppermute(x, "filt", [(i, i ^ 1) for i in range(size)])

    mine = near(pair)
    theirs = [swapped(x) for x in mine]
    dims = dict(depth=depth, height=height)
    again = call(join, shape(planes.shape, bf16), [anywhere, vmem], (mine[-1], planes), cost=12)
    behind = [shifted(planes, r, 0, size, count) for r in range(2, far)]
    behind = [planes, shifted(again, 1, 0, size, count)] + behind
    partial = call(
        functools.partial(own_parity, blocks=far, **dims),
        shape((depth * pairs, 3 * filters, 2 * across), f32),
        [vmem] * (1 + far) + [anywhere] * (far - 2),
        [w_mine, mine[-1]] + mine[:-1] + behind[2:],
        cost=28,
    )
    planes = call(
        join,
        shape((far * planes.shape[0], across), bf16),
        [anywhere] + [vmem] * far,
        [partial] + behind,
    ).reshape(-1, block, across)
    v = call(
        functools.partial(other_parity, **dims),
        shape((depth * height, filters, across), f32),
        [vmem] * (3 + far),
        [w_theirs, bias, partial] + theirs,
    )
    pooled = call(
        functools.partial(finish, count=count, **dims),
        shape((filters * depth * height // 4, across // 2), bf16),
        [vmem] * 5,
        (w_mine, w_theirs, v, planes, swapped(planes)),
    )
    return pooled.reshape(filters, depth // 2, height // 2, across // 2)


def solution(mesh):
    in_specs = (P("filt", "space", None, None), P("filt", None, None, None, None), P("filt"))
    out_specs = P("filt", "space", None, None)
    return jax.shard_map(
        on_device, mesh=mesh, in_specs=in_specs, out_specs=out_specs, check_vma=False
    )
```

```python
import functools

import jax
import jax.numpy as jnp
from jax import lax
from jax.experimental import pallas as pl
from jax.experimental.pallas import tpu as pltpu
from jax.sharding import PartitionSpec as P

slope = 0.3
f32, bf16 = jnp.float32, jnp.bfloat16


def one_hot(shape, wanted):
    target = lax.broadcasted_iota(jnp.int32, (shape[0], 1), 0)
    source = lax.broadcasted_iota(jnp.int32, shape, 1)
    return jnp.where(source == wanted(target), 1.0, 0.0).astype(bf16)


def pick_rows(x, block, count, first):
    rows = x.shape[0]
    cells = rows // block
    shift = block.bit_length() - 1
    pick = one_hot(
        (count * block, rows), lambda t: (t & (block - 1)) * cells + (t >> shift) + first
    )
    return jnp.dot(pick, x, preferred_element_type=f32).astype(bf16)


def begin(vol_ref, bias_ref, own_ref, *refs, block, depth, count):
    plane_refs, (bias_out_ref, done) = refs[:-2], refs[-2:]
    copies = [
        pltpu.make_async_copy(source, target, done.at[k])
        for k, (source, target) in enumerate(
            [(vol_ref, own_ref), (bias_ref, bias_out_ref)]
        )
    ]
    for copy in copies:
        copy.start()
    height = own_ref.shape[0] // block // depth
    last = (depth - 1) * height
    copies[0].wait()
    if count == 2:
        firsts = [jnp.where(lax.axis_index("space") == 0, last, 0)]
    else:
        firsts = [last, 0]
    for ref, first in zip(plane_refs, firsts):
        ref[...] = pick_rows(own_ref[...], block, height, first)
    for copy in copies[1:]:
        copy.wait()


def prepare(
    w_ref, bias_ref, w_mine_ref, w_theirs_ref, bias_out_ref, kernel_ref, done, *, block
):
    rows = w_ref.shape[0] // 9
    fetches = [
        pltpu.make_async_copy(
            w_ref.at[pl.ds(k * rows, rows)], kernel_ref.at[pl.ds(k * rows, rows)], done.at[k]
        )
        for k in range(9)
    ]
    for fetch in fetches:
        fetch.start()
    cin = kernel_ref.shape[-1]
    half = cin // 2
    far = half // block // 2
    shift = block.bit_length() - 1
    place = lax.axis_index("filt")
    core, group = place & 1, place >> 1
    source = lax.broadcasted_iota(jnp.int32, (cin, cin), 0)
    target = lax.broadcasted_iota(jnp.int32, (1, cin), 1)
    part = jnp.where(target < half, core, 1 - core)
    slot = (target & (half - 1)) >> shift
    relative = (slot >> 1) | jnp.where((slot & 1) > 0, far, 0)
    wanted = ((((relative ^ group) << 1) | part) << shift) | (target & (block - 1))
    shuffle = jnp.where(source == wanted, 1.0, 0.0).astype(bf16)
    filters = bias_ref.shape[1]
    row = lax.broadcasted_iota(jnp.int32, (filters, filters), 0)
    column = lax.broadcasted_iota(jnp.int32, (filters, filters), 1)
    spread = jnp.where(row == column, bias_ref[...].astype(f32), 0.0)
    bias_out_ref[...] = jnp.broadcast_to(
        jnp.sum(spread, axis=1, keepdims=True), bias_out_ref.shape
    )
    for fetch in fetches:
        fetch.wait()
    ordered = jnp.dot(kernel_ref[...], shuffle, preferred_element_type=f32).astype(bf16)
    w_mine_ref[...] = ordered[:, :half].reshape(w_mine_ref.shape)
    w_theirs_ref[...] = ordered[:, half:].reshape(w_theirs_ref.shape)


def assemble(_, own_ref, far_ref, pair_ref, *, block):
    size, across = own_ref.shape
    both = jnp.concatenate([own_ref[...], far_ref[...]], axis=1)
    moved = pick_rows(both, block, size // block, 0)
    pair_ref[:size] = moved[:, :across]
    pair_ref[size:] = moved[:, across:]


def join(*refs):
    in_refs, out_ref = refs[1:-1], refs[-1]
    at = 0
    for ref in in_refs:
        out_ref[at : at + ref.shape[0]] = ref[...]
        at += ref.shape[0]


def channels(refs, per_block, row):
    return jnp.concatenate(
        [ref[k * per_block + row] for ref in refs for k in range(ref.shape[0] // per_block)],
        axis=0,
    )


def windows(rows):
    zero = jnp.zeros_like(rows[0])
    rows = [zero] + rows + [zero]
    return [
        [jnp.concatenate([rows[y + b], rows[y + b + 1]], axis=1) for b in range(3)]
        for y in range(0, len(rows) - 2, 2)
    ]


def products(w_ref, refs, depth, height):
    cells = depth * height
    for z in range(depth):
        taps = [a for a in range(3) if 0 <= z + a - 1 < depth]
        left = jnp.concatenate([w_ref[a * 3 + b] for a in taps for b in range(3)], axis=1)
        views = [
            windows([channels(refs, cells, (z + a - 1) * height + y) for y in range(height)])
            for a in taps
        ]
        for y in range(height // 2):
            right = jnp.concatenate([w for view in views for w in view[y]], axis=0)
            yield z, y, jnp.dot(left, right, preferred_element_type=f32)


def combine(total, k, filters, across):
    part = total[:, k * across : (k + 1) * across]
    lane = lax.broadcasted_iota(jnp.int32, (filters, across), 1)
    left = pltpu.roll(part[:filters], 1, 1)
    right = pltpu.roll(part[2 * filters :], across - 1, 1)
    v = part[filters : 2 * filters]
    v += jnp.where(lane > 0, left, 0.0)
    return v + jnp.where(lane < across - 1, right, 0.0)


def own_parity(w_ref, *refs, depth, height, blocks):
    refs, sum_ref = (*refs[1:blocks], refs[0]), refs[-1]
    for z, y, total in products(w_ref, refs, depth, height):
        sum_ref[z * (height // 2) + y] = total


def other_parity(w_ref, bias_ref, sum_ref, *refs, depth, height):
    refs, v_ref = refs[:-1], refs[-1]
    filters, across = bias_ref.shape
    for z, y, total in products(w_ref, refs, depth, height):
        total += sum_ref[z * (height // 2) + y]
        for j in range(2):
            v_ref[z * height + 2 * y + j] = combine(total, j, filters, across) + bias_ref[...]


def finish(w_mine_ref, w_theirs_ref, v_ref, *refs, depth, height, count):
    refs, out_ref = refs[:-1], refs[-1]
    filters, across = v_ref.shape[1:]
    here = lax.axis_index("space")
    extra = 1 if count == 2 else 2
    beside = []
    for which in range(extra):
        tap = 2 * which if extra == 2 else jnp.where(here > 0, 0, 2)
        left = jnp.concatenate(
            [w[tap * 3 + b] for b in range(3) for w in (w_mine_ref, w_theirs_ref)], axis=1
        )
        rows = [channels(refs, extra * height, which * height + y) for y in range(height)]
        added = []
        for view in windows(rows):
            total = jnp.dot(left, jnp.concatenate(view, axis=0), preferred_element_type=f32)
            added += [combine(total, j, filters, across) for j in range(2)]
        beside.append(added)
    pooled = {}
    for z in range(depth):
        for y in range(height):
            v = v_ref[z * height + y]
            if z == 0:
                v += jnp.where(here > 0, beside[0][y], 0.0)
            if z == depth - 1:
                v += jnp.where(here < count - 1, beside[-1][y], 0.0)
            v = jnp.where(v > 0, v, slope * v)
            key = (z // 2, y // 2)
            pooled[key] = v if key not in pooled else jnp.maximum(pooled[key], v)
    stacked = jnp.concatenate(
        [pooled[z, y] for z in range(depth // 2) for y in range(height // 2)], axis=0
    )
    stacked = jnp.maximum(stacked, pltpu.roll(stacked, across - 1, 1)).astype(bf16)
    cells = (depth // 2) * (height // 2)
    size = cells * filters
    shift = cells.bit_length() - 1
    rows_pick = one_hot((size, size), lambda t: (t & (cells - 1)) * filters + (t >> shift))
    lane_from = lax.broadcasted_iota(jnp.int32, (across, across // 2), 0)
    lane_to = lax.broadcasted_iota(jnp.int32, (across, across // 2), 1)
    lanes_pick = jnp.where(lane_from == 2 * lane_to, 1.0, 0.0).astype(bf16)
    picked = jnp.dot(stacked, lanes_pick, preferred_element_type=f32).astype(bf16)
    out_ref[...] = jnp.dot(rows_pick, picked, preferred_element_type=f32).astype(bf16)


def shifted(x, relative, step, size, count):
    pairs = []
    for f in range(size):
        for s in range(count):
            t = 1 - s if step == "swap" else s + step
            if 0 <= t < count:
                pairs.append((f * count + s, (f ^ (2 * relative)) * count + t))
    return lax.ppermute(x, ("filt", "space"), pairs)


def on_device(volume, kernel, filter_bias):
    block, depth, height, across = volume.shape
    filters, cin = kernel.shape[0], kernel.shape[-1]
    size = lax.axis_size("filt")
    count = lax.axis_size("space")
    far = size // 4
    pairs = height // 2
    cells = depth * height * block
    beside = height * block
    steps = ["swap"] if count == 2 else [1, -1]
    extra = len(steps)

    vmem = pl.BlockSpec(memory_space=pltpu.VMEM)
    hbm = pl.BlockSpec(memory_space=pltpu.HBM)
    anywhere = pl.BlockSpec(memory_space=pl.ANY)
    shape = jax.ShapeDtypeStruct

    def call(body, outs, ins, args, scratch=(), cost=12):
        return pl.pallas_call(
            body,
            out_shape=outs,
            in_specs=ins,
            out_specs=jax.tree.map(lambda _: vmem, outs),
            scratch_shapes=scratch,
            compiler_params=pltpu.CompilerParams(vmem_limit_bytes=16 << 20),
            cost_estimate=pl.CostEstimate(flops=1 << cost, bytes_accessed=1 << 8, transcendentals=0),
        )(*args)

    def pinned(x):
        return pltpu.with_memory_space_constraint(x, pltpu.HBM)

    far_block = shifted(volume, far, 0, size, count)
    weights = kernel.transpose(1, 2, 3, 0, 4).reshape(-1, cin)
    own_block, *edges, bias = call(
        functools.partial(begin, block=block, depth=depth, count=count),
        [shape((cells, across), bf16)]
        + [shape((beside, across), bf16)] * extra
        + [shape((1, filters), bf16)],
        [hbm, hbm],
        (pinned(volume.reshape(cells, across)), pinned(filter_bias[None])),
        [pltpu.SemaphoreType.DMA((2,))],
    )
    sends = list(zip(edges, steps))
    far_planes = [shifted(x, far, step, size, count) for x, step in sends]
    own_planes = [shifted(x, 0, step, size, count) for x, step in sends]
    ordered = shape((9, 3 * filters, cin // 2), bf16)
    w_mine, w_theirs, bias = call(
        functools.partial(prepare, block=block),
        (ordered, ordered, shape((filters, across), f32)),
        [hbm, vmem],
        (pinned(weights), bias),
        [pltpu.VMEM(weights.shape, bf16), pltpu.SemaphoreType.DMA((9,))],
        cost=31,
    )

    pair = call(
        functools.partial(assemble, block=block),
        shape((2 * cells, across), bf16),
        [anywhere, vmem, vmem],
        (w_mine, own_block, far_block.reshape(cells, across)),
        cost=31,
    )
    planes = call(
        join,
        shape((2 * extra * beside, across), bf16),
        [anywhere] + [vmem] * (2 * extra),
        [pair] + own_planes + far_planes,
        cost=31,
    )

    def near(x):
        parts = {r: shifted(x, r, 0, size, count) for r in [far - 1, *range(1, far - 1)]}
        return [x.reshape(-1, block, across)] + [
            parts[r].reshape(-1, block, across) for r in range(1, far)
        ]

    def swapped(x):
        return lax.ppermute(x, "filt", [(i, i ^ 1) for i in range(size)])

    mine = near(pair)
    theirs = [swapped(x) for x in mine]
    dims = dict(depth=depth, height=height)
    again = call(join, shape(planes.shape, bf16), [anywhere, vmem], (mine[-1], planes), cost=12)
    behind = [shifted(planes, r, 0, size, count) for r in range(2, far)]
    behind = [planes, shifted(again, 1, 0, size, count)] + behind
    partial = call(
        functools.partial(own_parity, blocks=far, **dims),
        shape((depth * pairs, 3 * filters, 2 * across), f32),
        [vmem] * (1 + far) + [anywhere] * (far - 2),
        [w_mine, mine[-1]] + mine[:-1] + behind[:1:-1],
        cost=28,
    )
    planes = call(
        join,
        shape((far * planes.shape[0], across), bf16),
        [anywhere] + [vmem] * far,
        [partial] + behind,
    ).reshape(-1, block, across)
    v = call(
        functools.partial(other_parity, **dims),
        shape((depth * height, filters, across), f32),
        [vmem] * (3 + far),
        [w_theirs, bias, partial] + theirs,
    )
    pooled = call(
        functools.partial(finish, count=count, **dims),
        shape((filters * depth * height // 4, across // 2), bf16),
        [vmem] * 5,
        (w_mine, w_theirs, v, planes, swapped(planes)),
    )
    return pooled.reshape(filters, depth // 2, height // 2, across // 2)


def solution(mesh):
    in_specs = (P("filt", "space", None, None), P("filt", None, None, None, None), P("filt"))
    out_specs = P("filt", "space", None, None)
    return jax.shard_map(
        on_device, mesh=mesh, in_specs=in_specs, out_specs=out_specs, check_vma=False
    )
```

```python
import functools

import jax
import jax.numpy as jnp
from jax import lax
from jax.experimental import pallas as pl
from jax.experimental.pallas import tpu as pltpu
from jax.sharding import PartitionSpec as P

slope = 0.3
f32, bf16 = jnp.float32, jnp.bfloat16


def one_hot(shape, wanted):
    target = lax.broadcasted_iota(jnp.int32, (shape[0], 1), 0)
    source = lax.broadcasted_iota(jnp.int32, shape, 1)
    return jnp.where(source == wanted(target), 1.0, 0.0).astype(bf16)


def pick_rows(x, block, count, first):
    rows = x.shape[0]
    cells = rows // block
    shift = block.bit_length() - 1
    pick = one_hot(
        (count * block, rows), lambda t: (t & (block - 1)) * cells + (t >> shift) + first
    )
    return jnp.dot(pick, x, preferred_element_type=f32).astype(bf16)


def begin(vol_ref, bias_ref, own_ref, *refs, block, depth, count):
    plane_refs, (bias_out_ref, done) = refs[:-2], refs[-2:]
    copies = [
        pltpu.make_async_copy(source, target, done.at[k])
        for k, (source, target) in enumerate(
            [(vol_ref, own_ref), (bias_ref, bias_out_ref)]
        )
    ]
    for copy in copies:
        copy.start()
    height = own_ref.shape[0] // block // depth
    last = (depth - 1) * height
    copies[0].wait()
    if count == 2:
        firsts = [jnp.where(lax.axis_index("space") == 0, last, 0)]
    else:
        firsts = [last, 0]
    for ref, first in zip(plane_refs, firsts):
        ref[...] = pick_rows(own_ref[...], block, height, first)
    for copy in copies[1:]:
        copy.wait()


def prepare(
    w_ref, bias_ref, w_mine_ref, w_theirs_ref, bias_out_ref, kernel_ref, done, *, block
):
    rows = w_ref.shape[0] // 9
    fetches = [
        pltpu.make_async_copy(
            w_ref.at[pl.ds(k * rows, rows)], kernel_ref.at[pl.ds(k * rows, rows)], done.at[k]
        )
        for k in range(9)
    ]
    for fetch in fetches:
        fetch.start()
    cin = kernel_ref.shape[-1]
    half = cin // 2
    far = half // block // 2
    shift = block.bit_length() - 1
    place = lax.axis_index("filt")
    core, group = place & 1, place >> 1
    source = lax.broadcasted_iota(jnp.int32, (cin, cin), 0)
    target = lax.broadcasted_iota(jnp.int32, (1, cin), 1)
    part = jnp.where(target < half, core, 1 - core)
    slot = (target & (half - 1)) >> shift
    relative = (slot >> 1) | jnp.where((slot & 1) > 0, far, 0)
    wanted = ((((relative ^ group) << 1) | part) << shift) | (target & (block - 1))
    shuffle = jnp.where(source == wanted, 1.0, 0.0).astype(bf16)
    filters = bias_ref.shape[1]
    row = lax.broadcasted_iota(jnp.int32, (filters, filters), 0)
    column = lax.broadcasted_iota(jnp.int32, (filters, filters), 1)
    spread = jnp.where(row == column, bias_ref[...].astype(f32), 0.0)
    bias_out_ref[...] = jnp.broadcast_to(
        jnp.sum(spread, axis=1, keepdims=True), bias_out_ref.shape
    )
    for fetch in fetches:
        fetch.wait()
    ordered = jnp.dot(kernel_ref[...], shuffle, preferred_element_type=f32).astype(bf16)
    w_mine_ref[...] = ordered[:, :half].reshape(w_mine_ref.shape)
    w_theirs_ref[...] = ordered[:, half:].reshape(w_theirs_ref.shape)


def assemble(_, own_ref, far_ref, pair_ref, *, block):
    size, across = own_ref.shape
    both = jnp.concatenate([own_ref[...], far_ref[...]], axis=1)
    moved = pick_rows(both, block, size // block, 0)
    pair_ref[:size] = moved[:, :across]
    pair_ref[size:] = moved[:, across:]


def join(*refs):
    in_refs, out_ref = refs[1:-1], refs[-1]
    at = 0
    for ref in in_refs:
        out_ref[at : at + ref.shape[0]] = ref[...]
        at += ref.shape[0]


def channels(refs, per_block, row):
    return jnp.concatenate(
        [ref[k * per_block + row] for ref in refs for k in range(ref.shape[0] // per_block)],
        axis=0,
    )


def windows(rows):
    zero = jnp.zeros_like(rows[0])
    rows = [zero] + rows + [zero]
    return [
        [jnp.concatenate([rows[y + b], rows[y + b + 1]], axis=1) for b in range(3)]
        for y in range(0, len(rows) - 2, 2)
    ]


def products(w_ref, refs, depth, height):
    cells = depth * height
    for z in range(depth):
        taps = [a for a in range(3) if 0 <= z + a - 1 < depth]
        left = jnp.concatenate([w_ref[a * 3 + b] for a in taps for b in range(3)], axis=1)
        views = [
            windows([channels(refs, cells, (z + a - 1) * height + y) for y in range(height)])
            for a in taps
        ]
        for y in range(height // 2):
            right = jnp.concatenate([w for view in views for w in view[y]], axis=0)
            yield z, y, jnp.dot(left, right, preferred_element_type=f32)


def combine(total, k, filters, across):
    part = total[:, k * across : (k + 1) * across]
    lane = lax.broadcasted_iota(jnp.int32, (filters, across), 1)
    left = pltpu.roll(part[:filters], 1, 1)
    right = pltpu.roll(part[2 * filters :], across - 1, 1)
    v = part[filters : 2 * filters]
    v += jnp.where(lane > 0, left, 0.0)
    return v + jnp.where(lane < across - 1, right, 0.0)


def own_parity(w_ref, *refs, depth, height, blocks):
    refs, sum_ref = (*refs[1:blocks], refs[0]), refs[-1]
    for z, y, total in products(w_ref, refs, depth, height):
        sum_ref[z * (height // 2) + y] = total


def other_parity(w_ref, bias_ref, sum_ref, *refs, depth, height):
    refs, v_ref = refs[:-1], refs[-1]
    filters, across = bias_ref.shape
    for z, y, total in products(w_ref, refs, depth, height):
        total += sum_ref[z * (height // 2) + y]
        for j in range(2):
            v_ref[z * height + 2 * y + j] = combine(total, j, filters, across) + bias_ref[...]


def finish(w_mine_ref, w_theirs_ref, v_ref, *refs, depth, height, count):
    refs, out_ref = refs[:-1], refs[-1]
    filters, across = v_ref.shape[1:]
    here = lax.axis_index("space")
    extra = 1 if count == 2 else 2
    beside = []
    for which in range(extra):
        tap = 2 * which if extra == 2 else jnp.where(here > 0, 0, 2)
        left = jnp.concatenate(
            [w[tap * 3 + b] for b in range(3) for w in (w_mine_ref, w_theirs_ref)], axis=1
        )
        rows = [channels(refs, extra * height, which * height + y) for y in range(height)]
        added = []
        for view in windows(rows):
            total = jnp.dot(left, jnp.concatenate(view, axis=0), preferred_element_type=f32)
            added += [combine(total, j, filters, across) for j in range(2)]
        beside.append(added)
    pooled = {}
    for z in range(depth):
        for y in range(height):
            v = v_ref[z * height + y]
            if z == 0:
                v += jnp.where(here > 0, beside[0][y], 0.0)
            if z == depth - 1:
                v += jnp.where(here < count - 1, beside[-1][y], 0.0)
            v = jnp.where(v > 0, v, slope * v)
            key = (z // 2, y // 2)
            pooled[key] = v if key not in pooled else jnp.maximum(pooled[key], v)
    stacked = jnp.concatenate(
        [pooled[z, y] for z in range(depth // 2) for y in range(height // 2)], axis=0
    )
    stacked = jnp.maximum(stacked, pltpu.roll(stacked, across - 1, 1)).astype(bf16)
    cells = (depth // 2) * (height // 2)
    size = cells * filters
    shift = cells.bit_length() - 1
    rows_pick = one_hot((size, size), lambda t: (t & (cells - 1)) * filters + (t >> shift))
    lane_from = lax.broadcasted_iota(jnp.int32, (across, across // 2), 0)
    lane_to = lax.broadcasted_iota(jnp.int32, (across, across // 2), 1)
    lanes_pick = jnp.where(lane_from == 2 * lane_to, 1.0, 0.0).astype(bf16)
    picked = jnp.dot(stacked, lanes_pick, preferred_element_type=f32).astype(bf16)
    out_ref[...] = jnp.dot(rows_pick, picked, preferred_element_type=f32).astype(bf16)


def shifted(x, relative, step, size, count):
    pairs = []
    for f in range(size):
        for s in range(count):
            t = 1 - s if step == "swap" else s + step
            if 0 <= t < count:
                pairs.append((f * count + s, (f ^ (2 * relative)) * count + t))
    return lax.ppermute(x, ("filt", "space"), pairs)


def on_device(volume, kernel, filter_bias):
    block, depth, height, across = volume.shape
    filters, cin = kernel.shape[0], kernel.shape[-1]
    size = lax.axis_size("filt")
    count = lax.axis_size("space")
    far = size // 4
    pairs = height // 2
    cells = depth * height * block
    beside = height * block
    steps = ["swap"] if count == 2 else [1, -1]
    extra = len(steps)

    vmem = pl.BlockSpec(memory_space=pltpu.VMEM)
    hbm = pl.BlockSpec(memory_space=pltpu.HBM)
    anywhere = pl.BlockSpec(memory_space=pl.ANY)
    shape = jax.ShapeDtypeStruct

    def call(body, outs, ins, args, scratch=(), cost=12):
        return pl.pallas_call(
            body,
            out_shape=outs,
            in_specs=ins,
            out_specs=jax.tree.map(lambda _: vmem, outs),
            scratch_shapes=scratch,
            compiler_params=pltpu.CompilerParams(vmem_limit_bytes=16 << 20),
            cost_estimate=pl.CostEstimate(flops=1 << cost, bytes_accessed=1 << 8, transcendentals=0),
        )(*args)

    def pinned(x):
        return pltpu.with_memory_space_constraint(x, pltpu.HBM)

    far_block = shifted(volume, far, 0, size, count)
    weights = kernel.transpose(1, 2, 3, 0, 4).reshape(-1, cin)
    own_block, *edges, bias = call(
        functools.partial(begin, block=block, depth=depth, count=count),
        [shape((cells, across), bf16)]
        + [shape((beside, across), bf16)] * extra
        + [shape((1, filters), bf16)],
        [hbm, hbm],
        (pinned(volume.reshape(cells, across)), pinned(filter_bias[None])),
        [pltpu.SemaphoreType.DMA((2,))],
    )
    sends = list(zip(edges, steps))
    far_planes = [shifted(x, far, step, size, count) for x, step in sends]
    own_planes = [shifted(x, 0, step, size, count) for x, step in sends]
    ordered = shape((9, 3 * filters, cin // 2), bf16)
    w_mine, w_theirs, bias = call(
        functools.partial(prepare, block=block),
        (ordered, ordered, shape((filters, across), f32)),
        [hbm, vmem],
        (pinned(weights), bias),
        [pltpu.VMEM(weights.shape, bf16), pltpu.SemaphoreType.DMA((9,))],
        cost=31,
    )

    pair = call(
        functools.partial(assemble, block=block),
        shape((2 * cells, across), bf16),
        [anywhere, vmem, vmem],
        (w_mine, own_block, far_block.reshape(cells, across)),
        cost=31,
    )
    planes = call(
        join,
        shape((2 * extra * beside, across), bf16),
        [anywhere] + [vmem] * (2 * extra),
        [pair] + own_planes + far_planes,
        cost=31,
    )

    def near(x):
        parts = {r: shifted(x, r, 0, size, count) for r in [far - 1, *range(1, far - 1)]}
        return [x.reshape(-1, block, across)] + [
            parts[r].reshape(-1, block, across) for r in range(1, far)
        ]

    def swapped(x):
        return lax.ppermute(x, "filt", [(i, i ^ 1) for i in range(size)])

    mine = near(pair)
    theirs = [swapped(x) for x in mine]
    dims = dict(depth=depth, height=height)
    again = call(join, shape(planes.shape, bf16), [anywhere, vmem], (mine[-1], planes), cost=12)
    behind = [shifted(planes, r, 0, size, count) for r in range(2, far)]
    behind = [planes, shifted(again, 1, 0, size, count)] + behind
    partial = call(
        functools.partial(own_parity, blocks=far, **dims),
        shape((depth * pairs, 3 * filters, 2 * across), f32),
        [vmem] * (1 + far) + [anywhere] * (far - 3),
        [w_mine, mine[-1]] + mine[:-1] + behind[2:-1],
        cost=28,
    )
    planes = call(
        join,
        shape((far * planes.shape[0], across), bf16),
        [anywhere] + [vmem] * far,
        [partial] + behind,
    ).reshape(-1, block, across)
    v = call(
        functools.partial(other_parity, **dims),
        shape((depth * height, filters, across), f32),
        [vmem] * (3 + far),
        [w_theirs, bias, partial] + theirs,
    )
    pooled = call(
        functools.partial(finish, count=count, **dims),
        shape((filters * depth * height // 4, across // 2), bf16),
        [vmem] * 5,
        (w_mine, w_theirs, v, planes, swapped(planes)),
    )
    return pooled.reshape(filters, depth // 2, height // 2, across // 2)


def solution(mesh):
    in_specs = (P("filt", "space", None, None), P("filt", None, None, None, None), P("filt"))
    out_specs = P("filt", "space", None, None)
    return jax.shard_map(
        on_device, mesh=mesh, in_specs=in_specs, out_specs=out_specs, check_vma=False
    )
```

```python
import functools

import jax
import jax.numpy as jnp
from jax import lax
from jax.experimental import pallas as pl
from jax.experimental.pallas import tpu as pltpu
from jax.sharding import PartitionSpec as P

slope = 0.3
f32, bf16 = jnp.float32, jnp.bfloat16


def one_hot(shape, wanted):
    target = lax.broadcasted_iota(jnp.int32, (shape[0], 1), 0)
    source = lax.broadcasted_iota(jnp.int32, shape, 1)
    return jnp.where(source == wanted(target), 1.0, 0.0).astype(bf16)


def pick_rows(x, block, count, first):
    rows = x.shape[0]
    cells = rows // block
    shift = block.bit_length() - 1
    pick = one_hot(
        (count * block, rows), lambda t: (t & (block - 1)) * cells + (t >> shift) + first
    )
    return jnp.dot(pick, x, preferred_element_type=f32).astype(bf16)


def begin(vol_ref, bias_ref, own_ref, *refs, block, depth, count):
    plane_refs, (bias_out_ref, done) = refs[:-2], refs[-2:]
    copies = [
        pltpu.make_async_copy(source, target, done.at[k])
        for k, (source, target) in enumerate(
            [(vol_ref, own_ref), (bias_ref, bias_out_ref)]
        )
    ]
    for copy in copies:
        copy.start()
    height = own_ref.shape[0] // block // depth
    last = (depth - 1) * height
    copies[0].wait()
    if count == 2:
        firsts = [jnp.where(lax.axis_index("space") == 0, last, 0)]
    else:
        firsts = [last, 0]
    for ref, first in zip(plane_refs, firsts):
        ref[...] = pick_rows(own_ref[...], block, height, first)
    for copy in copies[1:]:
        copy.wait()


def prepare(
    w_ref, bias_ref, w_mine_ref, w_theirs_ref, bias_out_ref, kernel_ref, done, *, block
):
    rows = w_ref.shape[0] // 9
    fetches = [
        pltpu.make_async_copy(
            w_ref.at[pl.ds(k * rows, rows)], kernel_ref.at[pl.ds(k * rows, rows)], done.at[k]
        )
        for k in range(9)
    ]
    for fetch in fetches:
        fetch.start()
    cin = kernel_ref.shape[-1]
    half = cin // 2
    far = half // block // 2
    shift = block.bit_length() - 1
    place = lax.axis_index("filt")
    core, group = place & 1, place >> 1
    source = lax.broadcasted_iota(jnp.int32, (cin, cin), 0)
    target = lax.broadcasted_iota(jnp.int32, (1, cin), 1)
    part = jnp.where(target < half, core, 1 - core)
    slot = (target & (half - 1)) >> shift
    relative = (slot >> 1) | jnp.where((slot & 1) > 0, far, 0)
    wanted = ((((relative ^ group) << 1) | part) << shift) | (target & (block - 1))
    shuffle = jnp.where(source == wanted, 1.0, 0.0).astype(bf16)
    filters = bias_ref.shape[1]
    row = lax.broadcasted_iota(jnp.int32, (filters, filters), 0)
    column = lax.broadcasted_iota(jnp.int32, (filters, filters), 1)
    spread = jnp.where(row == column, bias_ref[...].astype(f32), 0.0)
    bias_out_ref[...] = jnp.broadcast_to(
        jnp.sum(spread, axis=1, keepdims=True), bias_out_ref.shape
    )
    for fetch in fetches:
        fetch.wait()
    ordered = jnp.dot(kernel_ref[...], shuffle, preferred_element_type=f32).astype(bf16)
    w_mine_ref[...] = ordered[:, :half].reshape(w_mine_ref.shape)
    w_theirs_ref[...] = ordered[:, half:].reshape(w_theirs_ref.shape)


def assemble(_, own_ref, far_ref, pair_ref, *, block):
    size, across = own_ref.shape
    both = jnp.concatenate([own_ref[...], far_ref[...]], axis=1)
    moved = pick_rows(both, block, size // block, 0)
    pair_ref[:size] = moved[:, :across]
    pair_ref[size:] = moved[:, across:]


def join(*refs):
    in_refs, out_ref = refs[1:-1], refs[-1]
    at = 0
    for ref in in_refs:
        out_ref[at : at + ref.shape[0]] = ref[...]
        at += ref.shape[0]


def join_turned(first, *refs):
    half = (len(refs) - 1) // 2
    join(first, *refs[half:-1], *refs[:half], refs[-1])


def channels(refs, per_block, row):
    return jnp.concatenate(
        [ref[k * per_block + row] for ref in refs for k in range(ref.shape[0] // per_block)],
        axis=0,
    )


def windows(rows):
    zero = jnp.zeros_like(rows[0])
    rows = [zero] + rows + [zero]
    return [
        [jnp.concatenate([rows[y + b], rows[y + b + 1]], axis=1) for b in range(3)]
        for y in range(0, len(rows) - 2, 2)
    ]


def products(w_ref, refs, depth, height):
    cells = depth * height
    for z in range(depth):
        taps = [a for a in range(3) if 0 <= z + a - 1 < depth]
        left = jnp.concatenate([w_ref[a * 3 + b] for a in taps for b in range(3)], axis=1)
        views = [
            windows([channels(refs, cells, (z + a - 1) * height + y) for y in range(height)])
            for a in taps
        ]
        for y in range(height // 2):
            right = jnp.concatenate([w for view in views for w in view[y]], axis=0)
            yield z, y, jnp.dot(left, right, preferred_element_type=f32)


def combine(total, k, filters, across):
    part = total[:, k * across : (k + 1) * across]
    lane = lax.broadcasted_iota(jnp.int32, (filters, across), 1)
    left = pltpu.roll(part[:filters], 1, 1)
    right = pltpu.roll(part[2 * filters :], across - 1, 1)
    v = part[filters : 2 * filters]
    v += jnp.where(lane > 0, left, 0.0)
    return v + jnp.where(lane < across - 1, right, 0.0)


def own_parity(w_ref, *refs, depth, height, blocks):
    refs, sum_ref = (*refs[1:blocks], refs[0]), refs[-1]
    for z, y, total in products(w_ref, refs, depth, height):
        sum_ref[z * (height // 2) + y] = total


def other_parity(w_ref, bias_ref, sum_ref, *refs, depth, height):
    refs, v_ref = refs[:-1], refs[-1]
    filters, across = bias_ref.shape
    for z, y, total in products(w_ref, refs, depth, height):
        total += sum_ref[z * (height // 2) + y]
        for j in range(2):
            v_ref[z * height + 2 * y + j] = combine(total, j, filters, across) + bias_ref[...]


def finish(w_mine_ref, w_theirs_ref, v_ref, *refs, depth, height, count):
    refs, out_ref = refs[:-1], refs[-1]
    filters, across = v_ref.shape[1:]
    here = lax.axis_index("space")
    extra = 1 if count == 2 else 2
    beside = []
    for which in range(extra):
        tap = 2 * which if extra == 2 else jnp.where(here > 0, 0, 2)
        left = jnp.concatenate(
            [w[tap * 3 + b] for b in range(3) for w in (w_mine_ref, w_theirs_ref)], axis=1
        )
        rows = [channels(refs, extra * height, which * height + y) for y in range(height)]
        added = []
        for view in windows(rows):
            total = jnp.dot(left, jnp.concatenate(view, axis=0), preferred_element_type=f32)
            added += [combine(total, j, filters, across) for j in range(2)]
        beside.append(added)
    pooled = {}
    for z in range(depth):
        for y in range(height):
            v = v_ref[z * height + y]
            if z == 0:
                v += jnp.where(here > 0, beside[0][y], 0.0)
            if z == depth - 1:
                v += jnp.where(here < count - 1, beside[-1][y], 0.0)
            v = jnp.where(v > 0, v, slope * v)
            key = (z // 2, y // 2)
            pooled[key] = v if key not in pooled else jnp.maximum(pooled[key], v)
    stacked = jnp.concatenate(
        [pooled[z, y] for z in range(depth // 2) for y in range(height // 2)], axis=0
    )
    stacked = jnp.maximum(stacked, pltpu.roll(stacked, across - 1, 1)).astype(bf16)
    cells = (depth // 2) * (height // 2)
    size = cells * filters
    shift = cells.bit_length() - 1
    rows_pick = one_hot((size, size), lambda t: (t & (cells - 1)) * filters + (t >> shift))
    lane_from = lax.broadcasted_iota(jnp.int32, (across, across // 2), 0)
    lane_to = lax.broadcasted_iota(jnp.int32, (across, across // 2), 1)
    lanes_pick = jnp.where(lane_from == 2 * lane_to, 1.0, 0.0).astype(bf16)
    picked = jnp.dot(stacked, lanes_pick, preferred_element_type=f32).astype(bf16)
    out_ref[...] = jnp.dot(rows_pick, picked, preferred_element_type=f32).astype(bf16)


def shifted(x, relative, step, size, count):
    pairs = []
    for f in range(size):
        for s in range(count):
            t = 1 - s if step == "swap" else s + step
            if 0 <= t < count:
                pairs.append((f * count + s, (f ^ (2 * relative)) * count + t))
    return lax.ppermute(x, ("filt", "space"), pairs)


def on_device(volume, kernel, filter_bias):
    block, depth, height, across = volume.shape
    filters, cin = kernel.shape[0], kernel.shape[-1]
    size = lax.axis_size("filt")
    count = lax.axis_size("space")
    far = size // 4
    pairs = height // 2
    cells = depth * height * block
    beside = height * block
    steps = ["swap"] if count == 2 else [1, -1]
    extra = len(steps)

    vmem = pl.BlockSpec(memory_space=pltpu.VMEM)
    hbm = pl.BlockSpec(memory_space=pltpu.HBM)
    anywhere = pl.BlockSpec(memory_space=pl.ANY)
    shape = jax.ShapeDtypeStruct

    def call(body, outs, ins, args, scratch=(), cost=12):
        return pl.pallas_call(
            body,
            out_shape=outs,
            in_specs=ins,
            out_specs=jax.tree.map(lambda _: vmem, outs),
            scratch_shapes=scratch,
            compiler_params=pltpu.CompilerParams(vmem_limit_bytes=16 << 20),
            cost_estimate=pl.CostEstimate(flops=1 << cost, bytes_accessed=1 << 8, transcendentals=0),
        )(*args)

    def pinned(x):
        return pltpu.with_memory_space_constraint(x, pltpu.HBM)

    far_block = shifted(volume, far, 0, size, count)
    weights = kernel.transpose(1, 2, 3, 0, 4).reshape(-1, cin)
    own_block, *edges, bias = call(
        functools.partial(begin, block=block, depth=depth, count=count),
        [shape((cells, across), bf16)]
        + [shape((beside, across), bf16)] * extra
        + [shape((1, filters), bf16)],
        [hbm, hbm],
        (pinned(volume.reshape(cells, across)), pinned(filter_bias[None])),
        [pltpu.SemaphoreType.DMA((2,))],
    )
    sends = list(zip(edges, steps))
    far_planes = [shifted(x, far, step, size, count) for x, step in sends]
    own_planes = [shifted(x, 0, step, size, count) for x, step in sends]
    ordered = shape((9, 3 * filters, cin // 2), bf16)
    w_mine, w_theirs, bias = call(
        functools.partial(prepare, block=block),
        (ordered, ordered, shape((filters, across), f32)),
        [hbm, vmem],
        (pinned(weights), bias),
        [pltpu.VMEM(weights.shape, bf16), pltpu.SemaphoreType.DMA((9,))],
        cost=31,
    )

    pair = call(
        functools.partial(assemble, block=block),
        shape((2 * cells, across), bf16),
        [anywhere, vmem, vmem],
        (w_mine, own_block, far_block.reshape(cells, across)),
        cost=31,
    )
    planes = call(
        join_turned,
        shape((2 * extra * beside, across), bf16),
        [anywhere] + [vmem] * (2 * extra),
        [pair] + far_planes + own_planes,
        cost=31,
    )

    def near(x):
        parts = {r: shifted(x, r, 0, size, count) for r in [far - 1, *range(1, far - 1)]}
        return [x.reshape(-1, block, across)] + [
            parts[r].reshape(-1, block, across) for r in range(1, far)
        ]

    def swapped(x):
        return lax.ppermute(x, "filt", [(i, i ^ 1) for i in range(size)])

    mine = near(pair)
    theirs = [swapped(x) for x in mine]
    dims = dict(depth=depth, height=height)
    again = call(join, shape(planes.shape, bf16), [anywhere, vmem], (mine[-1], planes), cost=12)
    behind = [shifted(planes, r, 0, size, count) for r in range(2, far)]
    behind = [planes, shifted(again, 1, 0, size, count)] + behind
    partial = call(
        functools.partial(own_parity, blocks=far, **dims),
        shape((depth * pairs, 3 * filters, 2 * across), f32),
        [vmem] * (1 + far) + [anywhere] * (far - 2),
        [w_mine, mine[-1]] + mine[:-1] + behind[2:],
        cost=28,
    )
    planes = call(
        join,
        shape((far * planes.shape[0], across), bf16),
        [anywhere] + [vmem] * far,
        [partial] + behind,
    ).reshape(-1, block, across)
    v = call(
        functools.partial(other_parity, **dims),
        shape((depth * height, filters, across), f32),
        [vmem] * (3 + far),
        [w_theirs, bias, partial] + theirs,
    )
    pooled = call(
        functools.partial(finish, count=count, **dims),
        shape((filters * depth * height // 4, across // 2), bf16),
        [vmem] * 5,
        (w_mine, w_theirs, v, planes, swapped(planes)),
    )
    return pooled.reshape(filters, depth // 2, height // 2, across // 2)


def solution(mesh):
    in_specs = (P("filt", "space", None, None), P("filt", None, None, None, None), P("filt"))
    out_specs = P("filt", "space", None, None)
    return jax.shard_map(
        on_device, mesh=mesh, in_specs=in_specs, out_specs=out_specs, check_vma=False
    )
```
